256 devices in a mesh: section: 8 (over x, y_lo), seq: 32 (over z, y_hi, core).
Axes of the slice: x: 4, y: 4 (y_hi: 2, y_lo: 2; y = y_hi * 2 + y_lo), z: 8, core: 2. Of those that a mesh axis runs over, the one named last changes fastest.
Arguments:
- queries: bfloat16 [8, 4096, 4096], P('section', 'seq'), may hold values from -6 to 6
- key_rows: bfloat16 [8, 4096, 512], P('section', 'seq'), may hold values from -6 to 6
- value_rows: bfloat16 [8, 4096, 512], P('section', 'seq'), may hold values from -6 to 6
- upstream: bfloat16 [8, 4096, 4096], P('section', 'seq'), may hold values from -6 to 6
- norm_gains: float32 [8, 256], P('section'), may hold values from 0.5 to 8, as said below
- segments: int32 [8, 4096], P('section'), may hold values from 0 to 5, never falling along the last dimension, each value on 1 to 1024 neighbouring positions
Outputs:
- attended: bfloat16 [8, 4096, 4096], P('section', 'seq')
- grad_queries: bfloat16 [8, 4096, 4096], P('section', 'seq')
- grad_keys: bfloat16 [8, 4096, 512], P('section', 'seq')
- grad_values: bfloat16 [8, 4096, 512], P('section', 'seq')
- grad_gains: float32 [8, 256], P('section')
The draws below stay inside these ranges and needn't reach their ends.
Inputs may be any that keep to these rules, and one draw needn't show every extreme that they name: `norm_gains`: row g of the gains equals row 7 - g. `segments`: document numbers never fall along a slab; a document spans at most 1024 tokens of it.
All inputs are finite; a program needn't handle non-finite values.
Results may differ from the reference program's by a relative error of at most 0.033.
The reference program's roundings to bfloat16 on the way (of `q_normed`, `k_normed`, `probs_b`, `d_scores` and `d_qn`) count: a program that leaves them out, or rounds other values in their place, can miss the bound.
Values may be sent and summed in bfloat16 or wider, within the bound.
A program may use at most 128 MiB of HBM per device.

```python
import math
import jax
import jax.numpy as jnp
import numpy as np
from jax import lax

SECTIONS = 8
TOKENS = 4096
SEQ_LEN = 2048
HEAD_DIM = 128
HEADS = 32
KV_HEADS = 4


def shared_keys(key):
    raw_keys = jax.random.normal(jax.random.fold_in(key, 101), (SECTIONS, TOKENS, KV_HEADS * HEAD_DIM), jnp.float32)
    return jnp.clip(raw_keys, -6.0, 6.0)


def draw_key_rows(key, part):
    base_key = key
    return shared_keys(base_key).astype(jnp.bfloat16)


def draw_queries(key, part):
    key = jax.random.fold_in(key, 5)
    raw_queries = jnp.clip(jax.random.normal(key, (SECTIONS, TOKENS, HEADS * HEAD_DIM), jnp.float32), -6.0, 6.0)
    return raw_queries.astype(jnp.bfloat16)


def draw_norm_gains(key, part):
    key = jax.random.fold_in(key, 7)
    base_gains = jnp.exp(jax.random.uniform(key, (SECTIONS, 2 * HEAD_DIM), jnp.float32, jnp.log(0.5), jnp.log(2.0)))
    section_ids = jnp.arange(SECTIONS)
    mirror_ids = jnp.minimum(section_ids, SECTIONS - 1 - section_ids)
    return base_gains[mirror_ids]


def block_levels(own_key, extent, pieces, low, largest):
    loudness, own = 1.0, jax.random.fold_in(own_key, 6)
    for axis_at, shards_of in pieces:
        steps = jnp.exp(jax.random.uniform(jax.random.fold_in(own, axis_at), (shards_of,), jnp.float32, low / len(pieces), largest / len(pieces)))
        loudness = loudness * jnp.repeat(steps, extent[axis_at] // shards_of).reshape([-1 if axis == axis_at else 1 for axis in range(len(extent))])
    return loudness


def profile(number_of, total, limit, skew):
    weights = [(1 << 20) // math.isqrt(grade ** skew) + 1 for grade in range(2, number_of + 1)]
    surplus, counts = total - limit - (number_of - 1), [1] * (number_of - 1)
    while surplus > 0:
        free = [i for i in range(number_of - 1) if counts[i] < limit]
        mass, remaining = sum([weights[i] for i in free]), surplus
        for i in free:
            extra = min(limit - counts[i], max(1, remaining * weights[i] // mass), surplus)
            counts[i] = counts[i] + extra
            surplus = surplus - extra
    return np.array([limit] + counts)


def uneven(rng, number_of, total, limit, skew):
    if number_of == 2:
        one = jax.random.randint(rng, (), max(1, total - limit), min(limit, total - 1) + 1)
        return jnp.stack([one, total - one])
    tallies = jnp.asarray(profile(number_of, total, limit, skew), jnp.int32)
    couples = (number_of - 1) // 2
    donor, receiver = tallies[1:1 + 2 * couples:2], tallies[2:2 + 2 * couples:2]
    room = jnp.minimum(donor - 1, limit - receiver)
    passed = jax.random.randint(jax.random.fold_in(rng, 1), (couples,), 0, 1 << 20) % (room + 1)
    tallies = tallies.at[1:1 + 2 * couples:2].set(donor - passed).at[2:2 + 2 * couples:2].set(receiver + passed)
    return tallies[jax.random.permutation(jax.random.fold_in(rng, 2), number_of)]


def gaussian(stream_key, dims, deviation, limit, shards=(), kind=jnp.bfloat16):
    array = deviation * jax.random.normal(stream_key, dims, jnp.float32)
    if shards:
        array = array * block_levels(stream_key, dims, shards, -0.22, 0.18)
    return jnp.clip(array, -limit, limit).astype(kind)


def setup_inputs(seed: int = 0) -> dict:
    splits = jax.random.split(jax.random.key(seed), 7)
    return {
        "queries": draw_queries(jax.random.fold_in(splits[6], 71), 0),
        "key_rows": draw_key_rows(jax.random.fold_in(splits[6], 71), 0),
        "value_rows": gaussian(splits[2], (SECTIONS, TOKENS, KV_HEADS * HEAD_DIM), 1.0, 6.0, ((0, 8), (1, 32))),
        "upstream": gaussian(splits[3], (SECTIONS, TOKENS, HEADS * HEAD_DIM), 1.0, 6.0, ((0, 8), (1, 32))),
        "norm_gains": draw_norm_gains(jax.random.fold_in(splits[6], 71), 0),
        "segments": jax.vmap(lambda own: jnp.searchsorted(jnp.cumsum(uneven(own, 3 * (TOKENS // SEQ_LEN), TOKENS, SEQ_LEN // 2, 0)), jnp.arange(TOKENS), side="right"))(jax.random.split(splits[5], SECTIONS)).reshape((SECTIONS, TOKENS)).astype(jnp.int32),
    }


epsilon = 1e-06

def unit_rows(raw):
    values_f = raw.astype(jnp.float32)
    root_mean = jnp.sqrt(lax.optimization_barrier(jnp.mean(values_f * values_f, axis=-1, keepdims=True)) + epsilon)
    return (values_f / root_mean, root_mean)

def head_pass(q_head, k_head, v_head, up_head, seg_ids):
    total = q_head.shape[0]
    width = q_head.shape[1]
    block = min(512, SEQ_LEN)
    factor = 1.0 / math.sqrt(width)
    out_blocks = []
    dq_blocks = []
    dk_blocks = []
    dv_blocks = []
    for seq_id in range(total // SEQ_LEN):
        seq_first = seq_id * SEQ_LEN
        dk_acc = jnp.zeros((SEQ_LEN, width), jnp.float32)
        dv_acc = jnp.zeros((SEQ_LEN, width), jnp.float32)
        for block_id in range(SEQ_LEN // block):
            first = seq_first + block_id * block
            last = first + block
            span = last - seq_first
            q_block = q_head[first:last]
            up_block = up_head[first:last]
            k_seen = k_head[seq_first:last]
            v_seen = v_head[seq_first:last]
            scores = jnp.dot(q_block, k_seen.T, preferred_element_type=jnp.float32) * factor
            row_pos = block_id * block + jnp.arange(block, dtype=jnp.int32)[:, None]
            col_pos = jnp.arange(span, dtype=jnp.int32)[None, :]
            allowed = (col_pos <= row_pos) & (seg_ids[first:last][:, None] == seg_ids[seq_first:last][None, :])
            scores = jnp.where(allowed, scores, -jnp.inf)
            top_score = lax.optimization_barrier(jnp.max(scores, axis=1, keepdims=True))
            weights = jnp.exp(scores - top_score)
            probs = weights / lax.optimization_barrier(jnp.sum(weights, axis=1, keepdims=True))
            probs_b = probs.astype(jnp.bfloat16)
            output_b = jnp.dot(probs_b, v_seen, preferred_element_type=jnp.float32).astype(jnp.bfloat16)
            delta = lax.optimization_barrier(jnp.sum(up_block.astype(jnp.float32) * output_b.astype(jnp.float32), axis=1, keepdims=True))
            d_probs = jnp.dot(up_block, v_seen.T, preferred_element_type=jnp.float32)
            d_scores = (probs * (d_probs - delta) * factor).astype(jnp.bfloat16)
            dq_blocks.append(jnp.dot(d_scores, k_seen, preferred_element_type=jnp.float32).astype(jnp.bfloat16))
            dk_part = jnp.dot(d_scores.T, q_block, preferred_element_type=jnp.float32)
            dv_part = jnp.dot(probs_b.T, up_block, preferred_element_type=jnp.float32)
            dk_acc = dk_acc + jnp.pad(dk_part, ((0, SEQ_LEN - span), (0, 0)))
            dv_acc = dv_acc + jnp.pad(dv_part, ((0, SEQ_LEN - span), (0, 0)))
            out_blocks.append(output_b)
        dk_blocks.append(dk_acc)
        dv_blocks.append(dv_acc)
    return (jnp.concatenate(out_blocks, 0), jnp.concatenate(dq_blocks, 0), jnp.concatenate(dk_blocks, 0), jnp.concatenate(dv_blocks, 0))

def one_section(operands):
    queries, key_rows, value_rows, upstream, norm_gains, segments = operands
    total = queries.shape[0]
    groups = HEADS // KV_HEADS
    gain_q = norm_gains[:HEAD_DIM]
    gain_k = norm_gains[HEAD_DIM:]
    q_unit, q_root = unit_rows(queries.reshape(total, HEADS, HEAD_DIM))
    k_unit, k_root = unit_rows(key_rows.reshape(total, KV_HEADS, HEAD_DIM))
    q_normed = (q_unit * gain_q).astype(jnp.bfloat16)
    k_normed = (k_unit * gain_k).astype(jnp.bfloat16)
    v_heads = value_rows.reshape(total, KV_HEADS, HEAD_DIM)
    up_heads = upstream.reshape(total, HEADS, HEAD_DIM)

    def per_head(head):
        kv_head = (head // groups).astype(jnp.int32)
        return head_pass(lax.dynamic_index_in_dim(q_normed, head, 1, keepdims=False), lax.dynamic_index_in_dim(k_normed, kv_head, 1, keepdims=False), lax.dynamic_index_in_dim(v_heads, kv_head, 1, keepdims=False), lax.dynamic_index_in_dim(up_heads, head, 1, keepdims=False), segments)
    out_h, dq_h, dk_h, dv_h = lax.map(per_head, jnp.arange(HEADS, dtype=jnp.int32))
    attended = out_h.transpose(1, 0, 2).reshape(total, HEADS * HEAD_DIM)
    dk_sum = dk_h.reshape(KV_HEADS, groups, total, HEAD_DIM).sum(axis=1).transpose(1, 0, 2)
    dv_sum = dv_h.reshape(KV_HEADS, groups, total, HEAD_DIM).sum(axis=1).transpose(1, 0, 2)
    d_qn = dq_h.transpose(1, 0, 2).astype(jnp.float32)
    scaled_q = d_qn * gain_q
    grad_q = ((scaled_q - q_unit * lax.optimization_barrier(jnp.mean(scaled_q * q_unit, axis=-1, keepdims=True))) / q_root).astype(jnp.bfloat16)
    scaled_k = dk_sum * gain_k
    grad_k = ((scaled_k - k_unit * lax.optimization_barrier(jnp.mean(scaled_k * k_unit, axis=-1, keepdims=True))) / k_root).astype(jnp.bfloat16)
    gain_terms = jnp.concatenate([lax.optimization_barrier(jnp.sum(d_qn * q_unit, axis=(0, 1))), lax.optimization_barrier(jnp.sum(dk_sum * k_unit, axis=(0, 1)))])
    return (attended, grad_q.reshape(total, HEADS * HEAD_DIM), grad_k.reshape(total, KV_HEADS * HEAD_DIM), dv_sum.astype(jnp.bfloat16).reshape(total, KV_HEADS * HEAD_DIM), gain_terms)

def reference(queries, key_rows, value_rows, upstream, norm_gains, segments):
    attended, grad_queries, grad_keys, grad_values, gain_terms = lax.map(one_section, (queries, key_rows, value_rows, upstream, norm_gains, segments))
    grad_gains = gain_terms + gain_terms[::-1]
    return (attended, grad_queries, grad_keys, grad_values, grad_gains)
```

```python
import functools
import math

import jax
import jax.numpy as jnp
from jax import lax
from jax.experimental import pallas as pl
from jax.experimental.pallas import tpu as pltpu
from jax.sharding import PartitionSpec as P

MESH = pl.DeviceIdType.MESH
HEAD_DIM = 128
GROUP = 8
ROWS = 128
PAIR = 2 * ROWS
SLOTS = 5
SPAN = SLOTS * PAIR
SEEN = SPAN - ROWS
EPSILON = 1e-06
FACTOR = 1.0 / math.sqrt(HEAD_DIM)
EXP2_FACTOR = FACTOR * math.log2(math.e)
MASKED = -1e30
F32 = jnp.float32
BF16 = jnp.bfloat16


def matmul(left, right, left_dim, right_dim):
    return lax.dot_general(
        left, right, (((left_dim,), (right_dim,)), ((), ())), preferred_element_type=F32
    )


def unit_rows(raw):
    values = raw.astype(F32)
    inverse = lax.rsqrt(jnp.mean(values * values, axis=-1, keepdims=True) + EPSILON)
    return values * inverse, inverse


def at_slot(slot):
    return pl.ds(pl.multiple_of(slot * PAIR, PAIR), PAIR)


def kernel(
    queries, keys, values, upstream, gains, segments,
    attended, grad_q, grad_k, grad_v, grad_gains,
    q_raw, up_raw, kv_raw, k_normed, k_unit_t, bias, acc,
    out_stage, kv_stage, y_out, z_out, y_in, z_in, gain_acc, gain_a, gain_b,
    local_sem, core_send, core_recv, gather_send, gather_recv,
    reduce_send, reduce_recv, out_sem, out_send, out_recv,
    kv_sem, kv_send, kv_recv, ga_send, ga_recv, gb_send, gb_recv,
):
    section = lax.axis_index("section")
    place = lax.axis_index("seq")
    core = place % 2
    col = (place // 2) % 2
    z = place // 4
    mirror = section // 4
    z_count = 8

    def device(z_at, col_at, core_at, section_at=None):
        return (section if section_at is None else section_at, (z_at * 2 + col_at) * 2 + core_at)

    sibling = device(z, col, 1 - core)
    across = device(z, 1 - col, core)
    up_z = device((z + 1) % z_count, col, core)
    down_z = device((z + z_count - 1) % z_count, col, core)

    def z_peer(step):
        return device((z + step) % z_count, col, core)

    def square_peer(code):
        flip_m, flip_h, flip_c = code // 4, (code // 2) % 2, code % 2
        return device(
            z,
            1 - col if flip_h else col,
            1 - core if flip_c else core,
            7 - section if flip_m else section,
        )

    barrier = pltpu.get_barrier_semaphore()
    for step in range(1, 8):
        pl.semaphore_signal(barrier, inc=1, device_id=z_peer(step), device_id_type=MESH)
        pl.semaphore_signal(barrier, inc=1, device_id=square_peer(step), device_id_type=MESH)

    def remote(src, dst, send, recv, target):
        return pltpu.make_async_remote_copy(
            src_ref=src, dst_ref=dst, send_sem=send, recv_sem=recv,
            device_id=target, device_id_type=MESH,
        )

    def q_columns(core_at, j):
        return pl.ds(pl.multiple_of(core_at * 2048 + j * 1024, 1024), 1024)

    def kv_columns(core_at, j):
        return pl.ds(pl.multiple_of(core_at * 256 + j * 128, 128), 128)

    def token_rows(core_at):
        return pl.ds(pl.multiple_of((SLOTS - 1) * PAIR + core_at * ROWS, ROWS), ROWS)

    def own_copy(kind, j):
        if kind < 2:
            source = (keys, values)[kind]
            return pltpu.make_async_copy(
                source.at[0, :, kv_columns(core, j)],
                kv_raw.at[j, kind, token_rows(core), :],
                local_sem.at[kind, j],
            )
        source, target = ((queries, q_raw), (upstream, up_raw))[kind - 2]
        return pltpu.make_async_copy(
            source.at[0, :, q_columns(core, j)],
            target.at[core, :, pl.ds(pl.multiple_of(j * 1024, 1024), 1024)],
            local_sem.at[kind, j],
        )

    def core_copy(kind, j):
        if kind < 2:
            source = (keys, values)[kind]
            return remote(
                source.at[0, :, kv_columns(1 - core, j)],
                kv_raw.at[j, kind, token_rows(core), :],
                core_send.at[kind, j],
                core_recv.at[kind, j],
                sibling,
            )
        source, target = ((queries, q_raw), (upstream, up_raw))[kind - 2]
        return remote(
            source.at[0, :, q_columns(1 - core, j)],
            target.at[core, :, pl.ds(pl.multiple_of(j * 1024, 1024), 1024)],
            core_send.at[kind, j],
            core_recv.at[kind, j],
            sibling,
        )

    def gather_copy(j, step):
        if step < 2:
            source, landing, target = 4 - 2 * step, 2 - 2 * step, up_z
        else:
            source, landing, target = 4 - 2 * (step - 2 + col), 3 - 2 * (step - 2), across
        return remote(
            kv_raw.at[j, :, at_slot(source), :],
            kv_raw.at[j, :, at_slot(landing), :],
            gather_send.at[j, step],
            gather_recv.at[j, step],
            target,
        )

    for j in range(2):
        for kind in range(2):
            own_copy(kind, j).start()
    for j in range(2):
        for kind in range(2, 4):
            own_copy(kind, j).start()
    pl.semaphore_wait(barrier, 14)
    for j in range(2):
        for kind in range(2):
            core_copy(kind, j).start()
    for j in range(2):
        for kind in range(2, 4):
            core_copy(kind, j).start()

    pair_at = z * 2 + col
    pieces = []
    for piece in range(SPAN // 128):
        at = jnp.maximum(pair_at * 2 - 8 + piece, 0)
        pieces.append(segments[:, pl.ds(pl.multiple_of(at * 128, 128), 128)].astype(F32))
    row_at = lax.broadcasted_iota(jnp.int32, (ROWS, SEEN), 0)
    key_at = lax.broadcasted_iota(jnp.int32, (ROWS, SEEN), 1)
    diagonal = lax.broadcasted_iota(jnp.int32, (ROWS, ROWS), 0) == lax.broadcasted_iota(
        jnp.int32, (ROWS, ROWS), 1
    )
    for r in range(2):
        row_segments = jnp.sum(jnp.where(diagonal, pieces[8 + r], 0.0), axis=1, keepdims=True)
        key_segments = jnp.concatenate(pieces[r : r + 9], axis=1)
        first_key = 1024 - r * ROWS - (pair_at % 8) * PAIR
        allowed = (
            (key_at <= row_at + 1024) & (key_at >= first_key) & (key_segments == row_segments)
        )
        bias[r] = jnp.where(allowed, 0.0, MASKED)

    acc[...] = jnp.zeros_like(acc)
    gain_acc[...] = jnp.zeros_like(gain_acc)

    for j in range(2):
        for kind in range(2):
            own_copy(kind, j).wait()
            core_copy(kind, j).wait_recv()
        gather_copy(j, 0).start()

        @pl.when(col == 0)
        def _():
            gather_copy(j, 2).start()

    for j in range(2):
        gather_copy(j, 0).wait_recv()
        gather_copy(j, 1).start()

        @pl.when(col == 0)
        def _():
            gather_copy(j, 3).start()

        @pl.when(col == 1)
        def _():
            gather_copy(j, 2).start()

    for j in range(2):
        gather_copy(j, 1).wait_recv()

        @pl.when(col == 1)
        def _():
            gather_copy(j, 3).start()

    gain_q = gains[:, :HEAD_DIM]
    gain_k = gains[:, HEAD_DIM:]

    def reduce_copy(j, step):
        if step < 2:
            buffer_out, buffer_in, target = z_out.at[j, step], z_in.at[j, step], down_z
        else:
            buffer_out, buffer_in, target = y_out.at[j, step - 2], y_in.at[j, step - 2], across
        return remote(
            buffer_out, buffer_in, reduce_send.at[j, step], reduce_recv.at[j, step], target
        )

    def send_sum(j, step, slot):
        if step < 2:
            z_out[j, step] = acc[j, :, :, at_slot(slot)].astype(BF16)
        else:
            y_out[j, step - 2] = acc[j, :, :, at_slot(slot)].astype(BF16)
        reduce_copy(j, step).start()

    def add_sum(j, step, slot):
        reduce_copy(j, step).wait_recv()
        term = z_in[j, step] if step < 2 else y_in[j, step - 2]
        acc[j, :, :, at_slot(slot)] += term.astype(F32)

    def reduce_first(j):
        send_sum(j, 3, 1)
        send_sum(j, 2, 3)

        @pl.when(col == 0)
        def _():
            send_sum(j, 0, 0)

    def reduce_second(j):
        add_sum(j, 3, 2 * (1 - col))

        @pl.when(col == 1)
        def _():
            send_sum(j, 0, 0)

    def reduce_third(j):
        add_sum(j, 2, 4 - 2 * col)
        add_sum(j, 0, 2)
        send_sum(j, 1, 2)

    def kv_copy(kind, j, r):
        target = (grad_k, grad_v)[kind].at[0, :, kv_columns(core, j)]
        if r is core:
            return pltpu.make_async_copy(kv_stage.at[j, kind, r], target, kv_sem.at[j, kind])
        return remote(
            kv_stage.at[j, kind, r], target, kv_send.at[j, kind], kv_recv.at[j, kind], sibling
        )

    other = 1 - core

    def reduce_last(j):
        add_sum(j, 1, 4)
        slot = at_slot(SLOTS - 1)
        d_key = acc[j, 0, :, slot].T
        d_value = acc[j, 1, :, slot].T
        k_unit, k_inverse = unit_rows(kv_raw[j, 0, slot, :])
        scaled = d_key * gain_k
        result = (
            scaled - k_unit * jnp.mean(scaled * k_unit, axis=-1, keepdims=True)
        ) * k_inverse
        kv_stage[j, 0] = result.astype(BF16).reshape(2, ROWS, HEAD_DIM)
        kv_stage[j, 1] = d_value.astype(BF16).reshape(2, ROWS, HEAD_DIM)
        for kind in range(2):
            kv_copy(kind, j, other).start()
            kv_copy(kind, j, core).start()

    def out_copy(kind, j, r):
        target = (attended, grad_q)[kind].at[0, :, q_columns(core, j)]
        source = out_stage.at[kind, r, :, pl.ds(pl.multiple_of(j * 1024, 1024), 1024)]
        if r is core:
            return pltpu.make_async_copy(source, target, out_sem.at[kind, j])
        return remote(source, target, out_send.at[kind, j], out_recv.at[kind, j], sibling)

    def attend(j, r):
        columns = [
            pl.ds(pl.multiple_of((j * GROUP + head) * HEAD_DIM, HEAD_DIM), HEAD_DIM)
            for head in range(GROUP)
        ]
        q_unit, q_inverse = unit_rows(jnp.concatenate([q_raw[r, :, at] for at in columns], 0))
        q = (q_unit * gain_q).astype(BF16)
        up = jnp.concatenate([up_raw[r, :, at] for at in columns], 0)
        seen = pl.ds(pl.multiple_of(r * ROWS, ROWS), SEEN)
        k = k_normed[j, seen, :]
        v = kv_raw[j, 1, seen, :]
        scores = matmul(q, k, 1, 1)
        d_probs = matmul(up, v, 1, 1)
        scores = (scores.reshape(GROUP, ROWS, SEEN) + bias[r][None]).reshape(GROUP * ROWS, SEEN)
        top = jnp.max(scores, axis=1, keepdims=True)
        weights = jnp.exp2((scores - top) * EXP2_FACTOR)
        probs = weights * (1.0 / jnp.sum(weights, axis=1, keepdims=True))
        probs_b = probs.astype(BF16)
        out = matmul(probs_b, v, 1, 0).astype(BF16)
        delta = jnp.sum(up.astype(F32) * out.astype(F32), axis=1, keepdims=True)
        d_scores = (probs * (d_probs - delta) * FACTOR).astype(BF16)
        d_qn = matmul(d_scores, k, 1, 0).astype(BF16).astype(F32)
        acc[j, 0, :, seen] += matmul(q, d_scores, 0, 0)
        acc[j, 1, :, seen] += matmul(up, probs_b, 0, 0)
        gain_acc[0] += jnp.sum((d_qn * q_unit).reshape(ROWS, GROUP, HEAD_DIM), axis=0)
        scaled = d_qn * gain_q
        d_query = (
            (scaled - q_unit * jnp.mean(scaled * q_unit, axis=-1, keepdims=True)) * q_inverse
        ).astype(BF16)
        for head, at in enumerate(columns):
            rows = slice(head * ROWS, (head + 1) * ROWS)
            out_stage[0, r, :, at] = out[rows]
            out_stage[1, r, :, at] = d_query[rows]

    def prepare(j):
        gather_copy(j, 2).wait_recv()
        gather_copy(j, 3).wait_recv()
        unit, _ = unit_rows(kv_raw[j, 0])
        k_normed[j] = (unit * gain_k).astype(BF16)
        k_unit_t[j] = unit.T

    def finish(j):
        product = acc[j, 0] * k_unit_t[j]
        total = product[:, :128]
        for piece in range(1, SPAN // 128):
            total = total + product[:, piece * 128 : (piece + 1) * 128]
        gain_acc[1] += jnp.sum(total.T.reshape(16, 8, HEAD_DIM), axis=0)

    def step(i, carry):
        j = i // 2

        @pl.when(i % 2 == 0)
        def _():
            for half in range(2):

                @pl.when(j == half)
                def _():
                    prepare(half)
                    for kind in range(2, 4):
                        core_copy(kind, half).wait_recv()

        @pl.when(i % 2 == 1)
        def _():
            for half in range(2):

                @pl.when(j == half)
                def _():
                    for kind in range(2, 4):
                        own_copy(kind, half).wait()

        attend(j, jnp.where(i % 2 == 0, other, core))

        @pl.when(i == 0)
        def _():
            for kind in range(2):
                out_copy(kind, 0, other).start()

        @pl.when(i == 1)
        def _():
            for kind in range(2):
                out_copy(kind, 0, core).start()
            finish(0)
            reduce_first(0)

        @pl.when(i == 2)
        def _():
            for kind in range(2):
                out_copy(kind, 1, other).start()
            reduce_second(0)

        @pl.when(i == 3)
        def _():
            for kind in range(2):
                out_copy(kind, 1, core).start()
            finish(1)
            reduce_first(1)

        return carry

    lax.fori_loop(0, 4, step, 0)

    def gain_a_copy(step):
        return remote(
            gain_a.at[0], gain_a.at[step], ga_send.at[step], ga_recv.at[step], z_peer(step)
        )

    def gain_b_copy(code):
        return remote(
            gain_b.at[0], gain_b.at[code], gb_send.at[code], gb_recv.at[code], square_peer(code)
        )

    gain_a[0, 0:1] = jnp.sum(gain_acc[0], axis=0, keepdims=True)
    gain_a[0, 1:2] = jnp.sum(gain_acc[1], axis=0, keepdims=True)
    gain_a[0, 2:8] = jnp.zeros((6, HEAD_DIM), F32)
    for at in range(1, 8):
        gain_a_copy(at).start()
    reduce_third(0)
    reduce_second(1)
    for at in range(1, 8):
        gain_a_copy(at).wait_recv()
    terms = gain_a[z % 8]
    for at in range(1, 8):
        terms = terms + gain_a[(z + 8 - at) % 8]
    gain_b[0] = terms
    for at in range(1, 8):
        gain_b_copy(at).start()
    reduce_last(0)
    reduce_third(1)
    reduce_last(1)
    for at in range(1, 8):
        gain_b_copy(at).wait_recv()
    sums = []
    for m in range(2):
        total = None
        for h in range(2):
            for c in range(2):
                term = gain_b[((mirror + m) % 2) * 4 + ((col + h) % 2) * 2 + (core + c) % 2]
                total = term if total is None else total + term
        sums.append(total)
    result = sums[0] + sums[1]
    grad_gains[:, :HEAD_DIM] = result[0:1]
    grad_gains[:, HEAD_DIM:] = result[1:2]

    for j in range(2):
        for kind in range(4):
            core_copy(kind, j).wait_send()
        for at in range(4):
            gather_copy(j, at).wait_send()
            reduce_copy(j, at).wait_send()
        for kind in range(2):
            out_copy(kind, j, core).wait()
            out_copy(kind, j, other).wait()
            kv_copy(kind, j, core).wait()
            kv_copy(kind, j, other).wait()
    for at in range(1, 8):
        gain_a_copy(at).wait_send()
        gain_b_copy(at).wait_send()


def on_device(queries, key_rows, value_rows, upstream, norm_gains, segments):
    any_space = pl.BlockSpec(memory_space=pl.ANY)
    vmem = pl.BlockSpec(memory_space=pltpu.VMEM)
    dma = pltpu.SemaphoreType.DMA
    return tuple(
        pl.pallas_call(
            kernel,
            out_shape=[
                jax.ShapeDtypeStruct(queries.shape, BF16),
                jax.ShapeDtypeStruct(queries.shape, BF16),
                jax.ShapeDtypeStruct(key_rows.shape, BF16),
                jax.ShapeDtypeStruct(key_rows.shape, BF16),
                jax.ShapeDtypeStruct(norm_gains.shape, F32),
            ],
            in_specs=[any_space] * 4 + [vmem] * 2,
            out_specs=[any_space] * 4 + [vmem],
            scratch_shapes=[
                pltpu.VMEM((2, ROWS, 2048), BF16),
                pltpu.VMEM((2, ROWS, 2048), BF16),
                pltpu.VMEM((2, 2, SPAN, HEAD_DIM), BF16),
                pltpu.VMEM((2, SPAN, HEAD_DIM), BF16),
                pltpu.VMEM((2, HEAD_DIM, SPAN), F32),
                pltpu.VMEM((2, ROWS, SEEN), F32),
                pltpu.VMEM((2, 2, HEAD_DIM, SPAN), F32),
                pltpu.VMEM((2, 2, ROWS, 2048), BF16),
                pltpu.VMEM((2, 2, 2, ROWS, HEAD_DIM), BF16),
                pltpu.VMEM((2, 2, 2, HEAD_DIM, PAIR), BF16),
                pltpu.VMEM((2, 2, 2, HEAD_DIM, PAIR), BF16),
                pltpu.VMEM((2, 2, 2, HEAD_DIM, PAIR), BF16),
                pltpu.VMEM((2, 2, 2, HEAD_DIM, PAIR), BF16),
                pltpu.VMEM((2, 8, HEAD_DIM), F32),
                pltpu.VMEM((8, 8, HEAD_DIM), F32),
                pltpu.VMEM((8, 8, HEAD_DIM), F32),
                dma((4, 2)),
                dma((4, 2)),
                dma((4, 2)),
                dma((2, 4)),
                dma((2, 4)),
                dma((2, 4)),
                dma((2, 4)),
                dma((2, 2)),
                dma((2, 2)),
                dma((2, 2)),
                dma((2, 2)),
                dma((2, 2)),
                dma((2, 2)),
                dma((8,)),
                dma((8,)),
                dma((8,)),
                dma((8,)),
            ],
            compiler_params=pltpu.CompilerParams(
                collective_id=0, has_side_effects=True, vmem_limit_bytes=56 * 2**20
            ),
            cost_estimate=pl.CostEstimate(
                flops=6 * 10**9, bytes_accessed=5 * 10**6, transcendentals=5 * 10**6
            ),
        )(queries, key_rows, value_rows, upstream, norm_gains, segments)
    )


def solution(mesh):
    rows = P("section", "seq", None)
    whole = P("section", None)
    return jax.shard_map(
        on_device,
        mesh=mesh,
        in_specs=(rows, rows, rows, rows, whole, whole),
        out_specs=(rows, rows, rows, rows, whole),
        check_vma=False,
    )
```

```python
import functools
import math

import jax
import jax.numpy as jnp
from jax import lax
from jax.experimental import pallas as pl
from jax.experimental.pallas import tpu as pltpu
from jax.sharding import PartitionSpec as P

MESH = pl.DeviceIdType.MESH
HEAD_DIM = 128
GROUP = 8
ROWS = 128
PAIR = 2 * ROWS
SLOTS = 5
SPAN = SLOTS * PAIR
SEEN = SPAN - ROWS
EPSILON = 1e-06
FACTOR = 1.0 / math.sqrt(HEAD_DIM)
EXP2_FACTOR = FACTOR * math.log2(math.e)
MASKED = -1e30
F32 = jnp.float32
BF16 = jnp.bfloat16


def matmul(left, right, left_dim, right_dim):
    return lax.dot_general(
        left, right, (((left_dim,), (right_dim,)), ((), ())), preferred_element_type=F32
    )


def unit_rows(raw):
    values = raw.astype(F32)
    inverse = lax.rsqrt(jnp.mean(values * values, axis=-1, keepdims=True) + EPSILON)
    return values * inverse, inverse


def at_slot(slot):
    return pl.ds(pl.multiple_of(slot * PAIR, PAIR), PAIR)


def kernel(
    queries, keys, values, upstream, gains, segments,
    attended, grad_q, grad_k, grad_v, grad_gains,
    q_raw, up_raw, kv_raw, q_normed, k_normed, k_unit_t, bias, acc,
    out_stage, kv_stage, sum_out, sum_in, gain_acc, gain_a, gain_b,
    local_sem, core_send, core_recv, gather_send, gather_recv,
    reduce_send, reduce_recv, out_sem, out_send, out_recv,
    kv_sem, kv_send, kv_recv, ga_send, ga_recv, gb_send, gb_recv,
):
    section = lax.axis_index("section")
    place = lax.axis_index("seq")
    core = place % 2
    col = (place // 2) % 2
    z = place // 4
    mirror = section // 4
    z_count = 8
    other = 1 - core
    gain_q = gains[:, :HEAD_DIM]
    gain_k = gains[:, HEAD_DIM:]

    def device(z_at, col_at, core_at, section_at=None):
        return (section if section_at is None else section_at, (z_at * 2 + col_at) * 2 + core_at)

    sibling = device(z, col, 1 - core)
    across = device(z, 1 - col, core)
    up_z = device((z + 1) % z_count, col, core)
    down_z = device((z + z_count - 1) % z_count, col, core)
    slant_up = device((z + col) % z_count, 1 - col, core)
    slant_down = device((z + z_count + col - 1) % z_count, 1 - col, core)
    slant = device((z + z_count + 2 * col - 1) % z_count, 1 - col, core)

    def z_peer(step):
        return device((z + step) % z_count, col, core)

    def square_peer(code):
        flip_m, flip_h, flip_c = code // 4, (code // 2) % 2, code % 2
        return device(
            z,
            1 - col if flip_h else col,
            1 - core if flip_c else core,
            7 - section if flip_m else section,
        )

    barrier = pltpu.get_barrier_semaphore()
    for step in range(1, 8):
        pl.semaphore_signal(barrier, inc=1, device_id=square_peer(step), device_id_type=MESH)
    for step in range(1, 8):
        pl.semaphore_signal(barrier, inc=1, device_id=z_peer(step), device_id_type=MESH)
    pl.semaphore_signal(barrier, inc=1, device_id=slant, device_id_type=MESH)

    def remote(src, dst, send, recv, target):
        return pltpu.make_async_remote_copy(
            src_ref=src, dst_ref=dst, send_sem=send, recv_sem=recv,
            device_id=target, device_id_type=MESH,
        )

    def q_columns(core_at, j):
        return pl.ds(pl.multiple_of(core_at * 2048 + j * 1024, 1024), 1024)

    def kv_columns(core_at, j):
        return pl.ds(pl.multiple_of(core_at * 256 + j * 128, 128), 128)

    def token_rows(core_at):
        return pl.ds(pl.multiple_of((SLOTS - 1) * PAIR + core_at * ROWS, ROWS), ROWS)

    def landing(kind, j):
        if kind < 2:
            return kv_raw.at[j, kind, token_rows(core), :]
        return (q_raw, up_raw)[kind - 2].at[core, :, pl.ds(j * 1024, 1024)]

    def leaving(kind, j, core_at):
        if kind < 2:
            return (keys, values)[kind].at[0, :, kv_columns(core_at, j)]
        return (queries, upstream)[kind - 2].at[0, :, q_columns(core_at, j)]

    def own_copy(kind, j):
        return pltpu.make_async_copy(
            leaving(kind, j, core), landing(kind, j), local_sem.at[kind, j]
        )

    def core_copy(kind, j):
        return remote(
            leaving(kind, j, other), landing(kind, j),
            core_send.at[kind, j], core_recv.at[kind, j], sibling,
        )

    def gather_copy(j, kind, step):
        if step < 2:
            source, target_slot, target = 4 - 2 * step, 2 - 2 * step, up_z
        elif step == 2:
            source, target_slot, target = 4 - 2 * col, 3, across
        else:
            source, target_slot, target = 2, 1, slant_up
        return remote(
            kv_raw.at[j, kind, at_slot(source), :],
            kv_raw.at[j, kind, at_slot(target_slot), :],
            gather_send.at[j, kind, step],
            gather_recv.at[j, kind, step],
            target,
        )

    def head_columns(j):
        return [
            slice((j * GROUP + head) * HEAD_DIM, (j * GROUP + head + 1) * HEAD_DIM)
            for head in range(GROUP)
        ]

    def stacked(ref, r, j):
        return jnp.concatenate([ref[r, :, at] for at in head_columns(j)], 0)

    def prepare_queries(j, r):
        unit, _ = unit_rows(stacked(q_raw, r, j))
        q_normed[j, r] = (unit * gain_q).astype(BF16)

    def prepare_keys(j, slot):
        rows = slice(slot * PAIR, (slot + 1) * PAIR)
        unit, _ = unit_rows(kv_raw[j, 0, rows, :])
        k_normed[j, rows, :] = (unit * gain_k).astype(BF16)
        k_unit_t[j, :, rows] = unit.T

    for kind in (2, 0, 1, 3):
        for j in range(2):
            own_copy(kind, j).start()

    pair_at = z * 2 + col
    pieces = []
    for piece in range(SPAN // 128):
        at = jnp.maximum(pair_at * 2 - 8 + piece, 0)
        pieces.append(segments[:, pl.ds(pl.multiple_of(at * 128, 128), 128)].astype(F32))
    row_at = lax.broadcasted_iota(jnp.int32, (ROWS, SEEN), 0)
    key_at = lax.broadcasted_iota(jnp.int32, (ROWS, SEEN), 1)
    diagonal = lax.broadcasted_iota(jnp.int32, (ROWS, ROWS), 0) == lax.broadcasted_iota(
        jnp.int32, (ROWS, ROWS), 1
    )
    for r in range(2):
        row_segments = jnp.sum(jnp.where(diagonal, pieces[8 + r], 0.0), axis=1, keepdims=True)
        key_segments = jnp.concatenate(pieces[r : r + 9], axis=1)
        first_key = 1024 - r * ROWS - (pair_at % 8) * PAIR
        allowed = (
            (key_at <= row_at + 1024) & (key_at >= first_key) & (key_segments == row_segments)
        )
        bias[r] = jnp.where(allowed, 0.0, MASKED)
    acc[...] = jnp.zeros_like(acc)
    gain_acc[...] = jnp.zeros_like(gain_acc)
    for j in range(2):
        own_copy(2, j).wait()
        prepare_queries(j, core)

    pl.semaphore_wait(barrier, 15)
    for j in range(2):
        for kind in range(2):
            core_copy(kind, j).start()
    for j in range(2):
        for kind in range(2, 4):
            core_copy(kind, j).start()
    for j in range(2):
        for kind in range(2):
            own_copy(kind, j).wait()
            core_copy(kind, j).wait_recv()
            gather_copy(j, kind, 0).start()

            @pl.when(col == 0)
            def _():
                gather_copy(j, kind, 2).start()

    for j in range(2):
        prepare_keys(j, 4)
    core_copy(2, 0).wait_recv()
    prepare_queries(0, other)
    for j in range(2):
        for kind in range(2):
            gather_copy(j, kind, 0).wait_recv()
            gather_copy(j, kind, 3).start()
            gather_copy(j, kind, 1).start()

            @pl.when(col == 1)
            def _():
                gather_copy(j, kind, 2).start()

    core_copy(2, 1).wait_recv()
    prepare_queries(1, other)
    for j in range(2):
        prepare_keys(j, 2)
        own_copy(3, j).wait()
        core_copy(3, j).wait_recv()

    def reduce_copy(j, kind, step):
        target = (down_z, down_z, across, slant_down)[step]
        return remote(
            sum_out.at[j, kind, step],
            sum_in.at[j, kind, step],
            reduce_send.at[j, kind, step],
            reduce_recv.at[j, kind, step],
            target,
        )

    def send_sum(j, kind, step, slot):
        sum_out[j, kind, step] = acc[j, kind, :, at_slot(slot)].astype(BF16)
        reduce_copy(j, kind, step).start()

    def add_sum(j, kind, step, slot):
        reduce_copy(j, kind, step).wait_recv()
        acc[j, kind, :, at_slot(slot)] += sum_in[j, kind, step].astype(F32)

    def reduce_first(j, kind):
        send_sum(j, kind, 3, 1)
        send_sum(j, kind, 0, 0)
        send_sum(j, kind, 2, 3)

    def reduce_second(j, kind):
        add_sum(j, kind, 3, 2)
        add_sum(j, kind, 0, 2)
        add_sum(j, kind, 2, 4 - 2 * col)
        send_sum(j, kind, 1, 2)

    def kv_copy(kind, j, r):
        target = (grad_k, grad_v)[kind].at[0, :, kv_columns(core, j)]
        if r is core:
            return pltpu.make_async_copy(kv_stage.at[j, kind, r], target, kv_sem.at[j, kind])
        return remote(
            kv_stage.at[j, kind, r], target, kv_send.at[j, kind], kv_recv.at[j, kind], sibling
        )

    def reduce_last(j, kind):
        add_sum(j, kind, 1, 4)
        slot = at_slot(SLOTS - 1)
        result = acc[j, kind, :, slot].T
        if kind == 0:
            k_unit, k_inverse = unit_rows(kv_raw[j, 0, slot, :])
            scaled = result * gain_k
            result = (
                scaled - k_unit * jnp.mean(scaled * k_unit, axis=-1, keepdims=True)
            ) * k_inverse
        kv_stage[j, kind] = result.astype(BF16).reshape(2, ROWS, HEAD_DIM)
        kv_copy(kind, j, other).start()
        kv_copy(kind, j, core).start()

    def out_copy(kind, j, r):
        target = (attended, grad_q)[kind].at[0, :, q_columns(core, j)]
        source = out_stage.at[kind, r, :, pl.ds(j * 1024, 1024)]
        if r is core:
            return pltpu.make_async_copy(source, target, out_sem.at[kind, j])
        return remote(source, target, out_send.at[kind, j], out_recv.at[kind, j], sibling)

    def attend(j, before_values, before_keys, after_keys):
        both = range(2)
        seen = [slice(r * ROWS, r * ROWS + SEEN) for r in both]
        q = [q_normed[j, r] for r in both]
        up = [stacked(up_raw, r, j) for r in both]
        k = [k_normed[j, seen[r], :] for r in both]
        v = [kv_raw[j, 1, seen[r], :] for r in both]
        scores, d_probs, probs, probs_b, delta, d_scores = ([None, None] for _ in range(6))

        def softmax(r):
            masked = scores[r].reshape(GROUP, ROWS, SEEN) + bias[r][None]
            masked = masked.reshape(GROUP * ROWS, SEEN)
            top = jnp.max(masked, axis=1, keepdims=True)
            weights = jnp.exp2((masked - top) * EXP2_FACTOR)
            probs[r] = weights * (1.0 / jnp.sum(weights, axis=1, keepdims=True))
            probs_b[r] = probs[r].astype(BF16)

        def output(r):
            out = matmul(probs_b[r], v[r], 1, 0).astype(BF16)
            delta[r] = jnp.sum(up[r].astype(F32) * out.astype(F32), axis=1, keepdims=True)
            for head, at in enumerate(head_columns(j)):
                out_stage[0, r, :, at] = out[head * ROWS : (head + 1) * ROWS]

        def score_gradient(r):
            d_scores[r] = (probs[r] * (d_probs[r] - delta[r]) * FACTOR).astype(BF16)

        def query_gradient(r):
            d_qn = matmul(d_scores[r], k[r], 1, 0).astype(BF16).astype(F32)
            q_unit, q_inverse = unit_rows(stacked(q_raw, r, j))
            gain_acc[0] += jnp.sum((d_qn * q_unit).reshape(ROWS, GROUP, HEAD_DIM), axis=0)
            scaled = d_qn * gain_q
            d_query = (
                (scaled - q_unit * jnp.mean(scaled * q_unit, axis=-1, keepdims=True)) * q_inverse
            ).astype(BF16)
            for head, at in enumerate(head_columns(j)):
                out_stage[1, r, :, at] = d_query[head * ROWS : (head + 1) * ROWS]

        for r in both:
            scores[r] = matmul(q[r], k[r], 1, 1)
        softmax(0)
        d_probs[0] = matmul(up[0], v[0], 1, 1)
        softmax(1)
        output(0)
        score_gradient(0)
        acc[j, 1, :, seen[0]] += matmul(up[0], probs_b[0], 0, 0)
        d_probs[1] = matmul(up[1], v[1], 1, 1)
        output(1)
        before_values()
        acc[j, 1, :, seen[1]] += matmul(up[1], probs_b[1], 0, 0)
        reduce_first(j, 1)
        score_gradient(1)
        acc[j, 0, :, seen[0]] += matmul(q[0], d_scores[0], 0, 0)
        before_keys()
        acc[j, 0, :, seen[1]] += matmul(q[1], d_scores[1], 0, 0)
        reduce_first(j, 0)
        after_keys()
        query_gradient(0)
        query_gradient(1)
        product = acc[j, 0] * k_unit_t[j]
        total = product[:, :128]
        for piece in range(1, SPAN // 128):
            total = total + product[:, piece * 128 : (piece + 1) * 128]
        gain_acc[1] += jnp.sum(total.T.reshape(16, 8, HEAD_DIM), axis=0)
        for kind in range(2):
            out_copy(kind, j, other).start()
            out_copy(kind, j, core).start()

    def arrive(j):
        for step in range(1, 4):
            for kind in range(2):
                gather_copy(j, kind, step).wait_recv()
        for slot in (0, 1, 3):
            prepare_keys(j, slot)

    def nothing():
        pass

    arrive(0)
    attend(0, nothing, nothing, nothing)
    arrive(1)
    attend(
        1,
        lambda: reduce_second(0, 1),
        lambda: reduce_second(0, 0),
        lambda: reduce_last(0, 1),
    )

    def gain_a_copy(step):
        return remote(
            gain_a.at[0], gain_a.at[step], ga_send.at[step], ga_recv.at[step], z_peer(step)
        )

    def gain_b_copy(code):
        return remote(
            gain_b.at[0], gain_b.at[code], gb_send.at[code], gb_recv.at[code], square_peer(code)
        )

    gain_a[0, 0:1] = jnp.sum(gain_acc[0], axis=0, keepdims=True)
    gain_a[0, 1:2] = jnp.sum(gain_acc[1], axis=0, keepdims=True)
    gain_a[0, 2:8] = jnp.zeros((6, HEAD_DIM), F32)
    for at in range(1, 8):
        gain_a_copy(at).start()
    reduce_second(1, 1)
    reduce_second(1, 0)
    reduce_last(0, 0)
    for at in range(1, 8):
        gain_a_copy(at).wait_recv()
    terms = gain_a[z % 8]
    for at in range(1, 8):
        terms = terms + gain_a[(z + 8 - at) % 8]
    gain_b[0] = terms
    for at in range(1, 8):
        gain_b_copy(at).start()
    reduce_last(1, 1)
    reduce_last(1, 0)
    for at in range(1, 8):
        gain_b_copy(at).wait_recv()
    sums = []
    for m in range(2):
        total = None
        for h in range(2):
            for c in range(2):
                term = gain_b[((mirror + m) % 2) * 4 + ((col + h) % 2) * 2 + (core + c) % 2]
                total = term if total is None else total + term
        sums.append(total)
    result = sums[0] + sums[1]
    grad_gains[:, :HEAD_DIM] = result[0:1]
    grad_gains[:, HEAD_DIM:] = result[1:2]

    for j in range(2):
        for kind in range(4):
            core_copy(kind, j).wait_send()
        for kind in range(2):
            for at in range(4):
                gather_copy(j, kind, at).wait_send()
                reduce_copy(j, kind, at).wait_send()
            out_copy(kind, j, core).wait()
            out_copy(kind, j, other).wait()
            kv_copy(kind, j, core).wait()
            kv_copy(kind, j, other).wait()
    for at in range(1, 8):
        gain_a_copy(at).wait_send()
        gain_b_copy(at).wait_send()


def hand_over(*refs):
    sources, targets, buffers, (in_sem, out_sem) = refs[:5], refs[5:10], refs[10:15], refs[15:]
    ways = []
    for at, (source, target, buffer) in enumerate(zip(sources, targets, buffers)):
        pieces = 4 if at < 2 else 1
        for piece in range(pieces):
            if len(source.shape) == 3:
                count = source.shape[1] // pieces
                view = (0, pl.ds(piece * count, count))
            else:
                view = (pl.ds(0, 1),)
            ways.append(
                (
                    pltpu.make_async_copy(
                        source.at[view], buffer.at[view], in_sem.at[at * 4 + piece]
                    ),
                    pltpu.make_async_copy(
                        buffer.at[view], target.at[view], out_sem.at[at * 4 + piece]
                    ),
                )
            )
    for inward, _ in ways:
        inward.start()
    for inward, outward in ways:
        inward.wait()
        outward.start()
    for _, outward in ways:
        outward.wait()


def on_device(queries, key_rows, value_rows, upstream, norm_gains, segments):
    any_space = pl.BlockSpec(memory_space=pl.ANY)
    vmem = pl.BlockSpec(memory_space=pltpu.VMEM)
    dma = pltpu.SemaphoreType.DMA
    shapes = [
        jax.ShapeDtypeStruct(queries.shape, BF16),
        jax.ShapeDtypeStruct(queries.shape, BF16),
        jax.ShapeDtypeStruct(key_rows.shape, BF16),
        jax.ShapeDtypeStruct(key_rows.shape, BF16),
        jax.ShapeDtypeStruct(norm_gains.shape, F32),
    ]
    results = pl.pallas_call(
        kernel,
        out_shape=shapes,
        in_specs=[any_space] * 4 + [vmem] * 2,
        out_specs=[any_space] * 4 + [vmem],
        scratch_shapes=[
            pltpu.VMEM((2, ROWS, 2048), BF16),
            pltpu.VMEM((2, ROWS, 2048), BF16),
            pltpu.VMEM((2, 2, SPAN, HEAD_DIM), BF16),
            pltpu.VMEM((2, 2, GROUP * ROWS, HEAD_DIM), BF16),
            pltpu.VMEM((2, SPAN, HEAD_DIM), BF16),
            pltpu.VMEM((2, HEAD_DIM, SPAN), F32),
            pltpu.VMEM((2, ROWS, SEEN), F32),
            pltpu.VMEM((2, 2, HEAD_DIM, SPAN), F32),
            pltpu.VMEM((2, 2, ROWS, 2048), BF16),
            pltpu.VMEM((2, 2, 2, ROWS, HEAD_DIM), BF16),
            pltpu.VMEM((2, 2, 4, HEAD_DIM, PAIR), BF16),
            pltpu.VMEM((2, 2, 4, HEAD_DIM, PAIR), BF16),
            pltpu.VMEM((2, 8, HEAD_DIM), F32),
            pltpu.VMEM((8, 8, HEAD_DIM), F32),
            pltpu.VMEM((8, 8, HEAD_DIM), F32),
            dma((4, 2)),
            dma((4, 2)),
            dma((4, 2)),
            dma((2, 2, 4)),
            dma((2, 2, 4)),
            dma((2, 2, 4)),
            dma((2, 2, 4)),
            dma((2, 2)),
            dma((2, 2)),
            dma((2, 2)),
            dma((2, 2)),
            dma((2, 2)),
            dma((2, 2)),
            dma((8,)),
            dma((8,)),
            dma((8,)),
            dma((8,)),
        ],
        compiler_params=pltpu.CompilerParams(
            collective_id=0, has_side_effects=True, vmem_limit_bytes=60 * 2**20
        ),
        cost_estimate=pl.CostEstimate(
            flops=6 * 10**9, bytes_accessed=5 * 10**6, transcendentals=5 * 10**6
        ),
    )(queries, key_rows, value_rows, upstream, norm_gains, segments)
    return tuple(
        pl.pallas_call(
            hand_over,
            out_shape=shapes,
            in_specs=[any_space] * 5,
            out_specs=[any_space] * 5,
            scratch_shapes=[pltpu.VMEM(one.shape, one.dtype) for one in shapes]
            + [dma((20,)), dma((20,))],
        )(*results)
    )


def solution(mesh):
    rows = P("section", "seq", None)
    whole = P("section", None)
    return jax.shard_map(
        on_device,
        mesh=mesh,
        in_specs=(rows, rows, rows, rows, whole, whole),
        out_specs=(rows, rows, rows, rows, whole),
        check_vma=False,
    )
```

```python
import functools
import math

import jax
import jax.numpy as jnp
from jax import lax
from jax.experimental import pallas as pl
from jax.experimental.pallas import tpu as pltpu
from jax.sharding import PartitionSpec as P

MESH = pl.DeviceIdType.MESH
HEAD_DIM = 128
GROUP = 8
ROWS = 128
PAIR = 2 * ROWS
SLOTS = 5
SPAN = SLOTS * PAIR
SEEN = SPAN - ROWS
EPSILON = 1e-06
FACTOR = 1.0 / math.sqrt(HEAD_DIM)
EXP2_FACTOR = FACTOR * math.log2(math.e)
MASKED = -1e30
F32 = jnp.float32
BF16 = jnp.bfloat16


def matmul(left, right, left_dim, right_dim):
    return lax.dot_general(
        left, right, (((left_dim,), (right_dim,)), ((), ())), preferred_element_type=F32
    )


def unit_rows(raw):
    values = raw.astype(F32)
    inverse = lax.rsqrt(jnp.mean(values * values, axis=-1, keepdims=True) + EPSILON)
    return values * inverse, inverse


def at_slot(slot):
    return pl.ds(pl.multiple_of(slot * PAIR, PAIR), PAIR)


def kernel(
    queries, keys, values, upstream, gains, segments,
    attended, grad_q, grad_k, grad_v, grad_gains,
    q_raw, up_raw, kv_raw, q_normed, k_normed, k_unit_t, bias, acc,
    out_stage, kv_stage, sum_out, sum_in, gain_acc, gain_a, gain_b,
    local_sem, core_send, core_recv, gather_send, gather_recv,
    reduce_send, reduce_recv, out_sem, out_send, out_recv,
    kv_sem, kv_send, kv_recv, ga_send, ga_recv, gb_send, gb_recv,
):
    section = lax.axis_index("section")
    place = lax.axis_index("seq")
    core = place % 2
    col = (place // 2) % 2
    z = place // 4
    mirror = section // 4
    z_count = 8
    other = 1 - core
    gain_q = gains[:, :HEAD_DIM]
    gain_k = gains[:, HEAD_DIM:]

    def device(z_at, col_at, core_at, section_at=None):
        return (section if section_at is None else section_at, (z_at * 2 + col_at) * 2 + core_at)

    sibling = device(z, col, 1 - core)
    across = device(z, 1 - col, core)
    up_z = device((z + 1) % z_count, col, core)
    down_z = device((z + z_count - 1) % z_count, col, core)
    slant_up = device((z + col) % z_count, 1 - col, core)
    slant_down = device((z + z_count + col - 1) % z_count, 1 - col, core)
    slant = device((z + z_count + 2 * col - 1) % z_count, 1 - col, core)

    up_cross = device((z + 1) % z_count, col, other)
    down_cross = device((z + z_count - 1) % z_count, col, other)

    def z_peer(step):
        return device((z + step) % z_count, col, core)

    def square_peer(code):
        flip_m, flip_h, flip_c = code // 4, (code // 2) % 2, code % 2
        return device(
            z,
            1 - col if flip_h else col,
            1 - core if flip_c else core,
            7 - section if flip_m else section,
        )

    barrier = pltpu.get_barrier_semaphore()
    for step in range(1, 8):
        pl.semaphore_signal(barrier, inc=1, device_id=square_peer(step), device_id_type=MESH)
    for step in range(1, 8):
        pl.semaphore_signal(barrier, inc=1, device_id=z_peer(step), device_id_type=MESH)
    for peer in (slant, up_cross, down_cross):
        pl.semaphore_signal(barrier, inc=1, device_id=peer, device_id_type=MESH)

    def remote(src, dst, send, recv, target):
        return pltpu.make_async_remote_copy(
            src_ref=src, dst_ref=dst, send_sem=send, recv_sem=recv,
            device_id=target, device_id_type=MESH,
        )

    def q_columns(core_at, j):
        return pl.ds(pl.multiple_of(core_at * 2048 + j * 1024, 1024), 1024)

    def kv_columns(core_at, j):
        return pl.ds(pl.multiple_of(core_at * 256 + j * 128, 128), 128)

    def token_rows(core_at):
        return pl.ds(pl.multiple_of((SLOTS - 1) * PAIR + core_at * ROWS, ROWS), ROWS)

    def landing(kind, j):
        if kind < 2:
            return kv_raw.at[j, kind, token_rows(core), :]
        return (q_raw, up_raw)[kind - 2].at[core, :, pl.ds(j * 1024, 1024)]

    def leaving(kind, j, core_at):
        if kind < 2:
            return (keys, values)[kind].at[0, :, kv_columns(core_at, j)]
        return (queries, upstream)[kind - 2].at[0, :, q_columns(core_at, j)]

    def own_copy(kind, j):
        return pltpu.make_async_copy(
            leaving(kind, j, core), landing(kind, j), local_sem.at[kind, j]
        )

    def core_copy(kind, j):
        return remote(
            leaving(kind, j, other), landing(kind, j),
            core_send.at[kind, j], core_recv.at[kind, j], sibling,
        )

    def gather_copy(j, kind, step):
        if step < 2:
            source, target_slot, target = 4 - 2 * step, 2 - 2 * step, up_z
        elif step == 2:
            source, target_slot, target = 4 - 2 * col, 3, across
        else:
            source, target_slot, target = 2, 1, slant_up
        return remote(
            kv_raw.at[j, kind, at_slot(source), :],
            kv_raw.at[j, kind, at_slot(target_slot), :],
            gather_send.at[j, kind, step],
            gather_recv.at[j, kind, step],
            target,
        )

    def head_columns(j):
        return [
            slice((j * GROUP + head) * HEAD_DIM, (j * GROUP + head + 1) * HEAD_DIM)
            for head in range(GROUP)
        ]

    def stacked(ref, r, j):
        return jnp.concatenate([ref[r, :, at] for at in head_columns(j)], 0)

    def prepare_queries(j, r):
        unit, _ = unit_rows(stacked(q_raw, r, j))
        q_normed[j, r] = (unit * gain_q).astype(BF16)

    def prepare_keys(j, slot):
        rows = slice(slot * PAIR, (slot + 1) * PAIR)
        unit, _ = unit_rows(kv_raw[j, 0, rows, :])
        k_normed[j, rows, :] = (unit * gain_k).astype(BF16)
        k_unit_t[j, :, rows] = unit.T

    for kind in (2, 0, 1, 3):
        for j in range(2):
            own_copy(kind, j).start()

    pair_at = z * 2 + col
    pieces = []
    for piece in range(SPAN // 128):
        at = jnp.maximum(pair_at * 2 - 8 + piece, 0)
        pieces.append(segments[:, pl.ds(pl.multiple_of(at * 128, 128), 128)].astype(F32))
    row_at = lax.broadcasted_iota(jnp.int32, (ROWS, SEEN), 0)
    key_at = lax.broadcasted_iota(jnp.int32, (ROWS, SEEN), 1)
    diagonal = lax.broadcasted_iota(jnp.int32, (ROWS, ROWS), 0) == lax.broadcasted_iota(
        jnp.int32, (ROWS, ROWS), 1
    )
    for r in range(2):
        row_segments = jnp.sum(jnp.where(diagonal, pieces[8 + r], 0.0), axis=1, keepdims=True)
        key_segments = jnp.concatenate(pieces[r : r + 9], axis=1)
        first_key = 1024 - r * ROWS - (pair_at % 8) * PAIR
        allowed = (
            (key_at <= row_at + 1024) & (key_at >= first_key) & (key_segments == row_segments)
        )
        bias[r] = jnp.where(allowed, 0.0, MASKED)
    acc[...] = jnp.zeros_like(acc)
    gain_acc[...] = jnp.zeros_like(gain_acc)
    for j in range(2):
        own_copy(2, j).wait()
        prepare_queries(j, core)

    def first_copy(kind, cross):
        rows = pl.ds(pl.multiple_of(2 * PAIR + core * ROWS, ROWS), ROWS)
        return remote(
            leaving(kind, 0, other if cross else core),
            kv_raw.at[0, kind, rows, :],
            gather_send.at[0, kind, 4 * cross],
            gather_recv.at[0, kind, 4 * cross],
            up_cross if cross else up_z,
        )

    def enter(j, kind):
        own_copy(kind, j).wait()
        core_copy(kind, j).wait_recv()
        if j == 1:
            gather_copy(j, kind, 0).start()

    def pass_on(j, kind):
        if j == 0:
            first_copy(kind, 0).wait_recv()
            first_copy(kind, 1).wait_recv()
        else:
            gather_copy(j, kind, 0).wait_recv()
        gather_copy(j, kind, 1).start()
        gather_copy(j, kind, 3).start()

    pl.semaphore_wait(barrier, 17)
    for kind in range(2):
        for cross in range(2):
            first_copy(kind, cross).start()
    for j in range(2):
        for kind in range(2):
            core_copy(kind, j).start()
    for j in range(2):
        for kind in range(2, 4):
            core_copy(kind, j).start()
    for kind in range(2):
        enter(0, kind)

        @pl.when(col == 0)
        def _():
            gather_copy(0, kind, 2).start()

    prepare_keys(0, 4)
    pass_on(0, 0)

    @pl.when(col == 1)
    def _():
        gather_copy(0, 0, 2).start()

    enter(1, 0)
    pass_on(0, 1)

    @pl.when(col == 1)
    def _():
        gather_copy(0, 1, 2).start()

    enter(1, 1)
    prepare_keys(0, 2)
    prepare_keys(1, 4)
    core_copy(2, 0).wait_recv()
    prepare_queries(0, other)
    core_copy(2, 1).wait_recv()
    prepare_queries(1, other)

    def reduce_copy(j, kind, step):
        target = (down_z, down_z, across, slant_down)[step]
        return remote(
            sum_out.at[j, kind, step],
            sum_in.at[j, kind, step],
            reduce_send.at[j, kind, step],
            reduce_recv.at[j, kind, step],
            target,
        )

    def send_sum(j, kind, step, slot):
        sum_out[j, kind, step] = acc[j, kind, :, at_slot(slot)].astype(BF16)
        reduce_copy(j, kind, step).start()

    def add_sum(j, kind, step, slot):
        reduce_copy(j, kind, step).wait_recv()
        acc[j, kind, :, at_slot(slot)] += sum_in[j, kind, step].astype(F32)

    def reduce_first(j, kind):
        send_sum(j, kind, 3, 1)
        send_sum(j, kind, 0, 0)
        send_sum(j, kind, 2, 3)

    def reduce_second(j, kind):
        add_sum(j, kind, 3, 2)
        add_sum(j, kind, 0, 2)
        add_sum(j, kind, 2, 4 - 2 * col)
        send_sum(j, kind, 1, 2)

    def kv_copy(kind, j, r):
        target = (grad_k, grad_v)[kind].at[0, :, kv_columns(core, j)]
        if r is core:
            return pltpu.make_async_copy(kv_stage.at[j, kind, r], target, kv_sem.at[j, kind])
        return remote(
            kv_stage.at[j, kind, r], target, kv_send.at[j, kind], kv_recv.at[j, kind], sibling
        )

    def reduce_last(j, kind):
        add_sum(j, kind, 1, 4)
        slot = at_slot(SLOTS - 1)
        result = acc[j, kind, :, slot].T
        if kind == 0:
            k_unit, k_inverse = unit_rows(kv_raw[j, 0, slot, :])
            scaled = result * gain_k
            result = (
                scaled - k_unit * jnp.mean(scaled * k_unit, axis=-1, keepdims=True)
            ) * k_inverse
        kv_stage[j, kind] = result.astype(BF16).reshape(2, ROWS, HEAD_DIM)
        kv_copy(kind, j, other).start()
        kv_copy(kind, j, core).start()

    def out_copy(kind, j, r):
        target = (attended, grad_q)[kind].at[0, :, q_columns(core, j)]
        source = out_stage.at[kind, r, :, pl.ds(j * 1024, 1024)]
        if r is core:
            return pltpu.make_async_copy(source, target, out_sem.at[kind, j])
        return remote(source, target, out_send.at[kind, j], out_recv.at[kind, j], sibling)

    def attend(j, before_values, after_values, after_keys, after_gains):
        both = range(2)
        seen = [slice(r * ROWS, r * ROWS + SEEN) for r in both]
        q = [q_normed[j, r] for r in both]
        k = [k_normed[j, seen[r], :] for r in both]
        scores, d_probs, probs, probs_b, delta, d_scores = ([None, None] for _ in range(6))

        up = v = None

        def softmax(r):
            masked = scores[r].reshape(GROUP, ROWS, SEEN) + bias[r][None]
            masked = masked.reshape(GROUP * ROWS, SEEN)
            top = jnp.max(masked, axis=1, keepdims=True)
            weights = jnp.exp2((masked - top) * EXP2_FACTOR)
            probs[r] = weights * (1.0 / jnp.sum(weights, axis=1, keepdims=True))
            probs_b[r] = probs[r].astype(BF16)

        def output(r):
            out = matmul(probs_b[r], v[r], 1, 0).astype(BF16)
            delta[r] = jnp.sum(up[r].astype(F32) * out.astype(F32), axis=1, keepdims=True)
            for head, at in enumerate(head_columns(j)):
                out_stage[0, r, :, at] = out[head * ROWS : (head + 1) * ROWS]

        def score_gradient(r):
            d_scores[r] = (probs[r] * (d_probs[r] - delta[r]) * FACTOR).astype(BF16)

        def query_gradient(r):
            d_qn = matmul(d_scores[r], k[r], 1, 0).astype(BF16).astype(F32)
            q_unit, q_inverse = unit_rows(stacked(q_raw, r, j))
            gain_acc[0] += jnp.sum((d_qn * q_unit).reshape(ROWS, GROUP, HEAD_DIM), axis=0)
            scaled = d_qn * gain_q
            d_query = (
                (scaled - q_unit * jnp.mean(scaled * q_unit, axis=-1, keepdims=True)) * q_inverse
            ).astype(BF16)
            for head, at in enumerate(head_columns(j)):
                out_stage[1, r, :, at] = d_query[head * ROWS : (head + 1) * ROWS]

        for r in both:
            scores[r] = matmul(q[r], k[r], 1, 1)
        softmax(0)
        before_values()
        up = [stacked(up_raw, r, j) for r in both]
        v = [kv_raw[j, 1, seen[r], :] for r in both]
        d_probs[0] = matmul(up[0], v[0], 1, 1)
        softmax(1)
        output(0)
        score_gradient(0)
        acc[j, 1, :, seen[0]] += matmul(up[0], probs_b[0], 0, 0)
        d_probs[1] = matmul(up[1], v[1], 1, 1)
        output(1)
        acc[j, 1, :, seen[1]] += matmul(up[1], probs_b[1], 0, 0)
        after_values()
        score_gradient(1)
        acc[j, 0, :, seen[0]] += matmul(q[0], d_scores[0], 0, 0)
        acc[j, 0, :, seen[1]] += matmul(q[1], d_scores[1], 0, 0)
        after_keys()
        query_gradient(0)
        query_gradient(1)
        product = acc[j, 0] * k_unit_t[j]
        total = product[:, :128]
        for piece in range(1, SPAN // 128):
            total = total + product[:, piece * 128 : (piece + 1) * 128]
        gain_acc[1] += jnp.sum(total.T.reshape(16, 8, HEAD_DIM), axis=0)
        after_gains()
        for kind in (1, 0):
            out_copy(kind, j, other).start()
            out_copy(kind, j, core).start()

    def arrive(j, kind, slots=()):
        for step in range(1, 4):
            gather_copy(j, kind, step).wait_recv()
        for slot in slots:
            prepare_keys(j, slot)

    def pass_across(kind):
        pass_on(1, kind)
        gather_copy(1, kind, 2).start()

    def first_values():
        own_copy(3, 0).wait()
        core_copy(3, 0).wait_recv()
        pass_across(0)
        arrive(0, 1)

    def second_values():
        own_copy(3, 1).wait()
        core_copy(3, 1).wait_recv()
        arrive(1, 1)

    def gain_a_copy(step):
        return remote(
            gain_a.at[0], gain_a.at[step], ga_send.at[step], ga_recv.at[step], z_peer(step)
        )

    def gain_b_copy(code):
        return remote(
            gain_b.at[0], gain_b.at[code], gb_send.at[code], gb_recv.at[code], square_peer(code)
        )

    def send_gains():
        gain_a[0, 0:1] = jnp.sum(gain_acc[0], axis=0, keepdims=True)
        gain_a[0, 1:2] = jnp.sum(gain_acc[1], axis=0, keepdims=True)
        gain_a[0, 2:8] = jnp.zeros((6, HEAD_DIM), F32)
        for at in range(1, 8):
            gain_a_copy(at).start()

    def nothing():
        pass

    def first_sums():
        reduce_first(0, 1)
        reduce_first(0, 0)

    def value_sums():
        reduce_second(0, 1)
        reduce_first(1, 1)

    def key_sums():
        reduce_first(1, 0)
        reduce_second(0, 0)

    arrive(0, 0, (0, 1, 3))
    attend(0, first_values, lambda: pass_across(1), first_sums, nothing)
    arrive(1, 0, (0, 1, 2, 3))
    attend(1, second_values, value_sums, key_sums, send_gains)
    reduce_last(0, 1)
    reduce_second(1, 1)
    reduce_last(0, 0)
    reduce_second(1, 0)
    for at in range(1, 8):
        gain_a_copy(at).wait_recv()
    terms = gain_a[z % 8]
    for at in range(1, 8):
        terms = terms + gain_a[(z + 8 - at) % 8]
    gain_b[0] = terms
    for at in range(1, 8):
        gain_b_copy(at).start()
    reduce_last(1, 1)
    reduce_last(1, 0)
    for at in range(1, 8):
        gain_b_copy(at).wait_recv()
    sums = []
    for m in range(2):
        total = None
        for h in range(2):
            for c in range(2):
                term = gain_b[((mirror + m) % 2) * 4 + ((col + h) % 2) * 2 + (core + c) % 2]
                total = term if total is None else total + term
        sums.append(total)
    result = sums[0] + sums[1]
    grad_gains[:, :HEAD_DIM] = result[0:1]
    grad_gains[:, HEAD_DIM:] = result[1:2]

    for j in range(2):
        for kind in range(4):
            core_copy(kind, j).wait_send()
        for kind in range(2):
            for at in range(4):
                if j == 0 and at == 0:
                    first_copy(kind, 0).wait_send()
                    first_copy(kind, 1).wait_send()
                else:
                    gather_copy(j, kind, at).wait_send()
                reduce_copy(j, kind, at).wait_send()
            out_copy(kind, j, core).wait()
            out_copy(kind, j, other).wait()
            kv_copy(kind, j, core).wait()
            kv_copy(kind, j, other).wait()
    for at in range(1, 8):
        gain_a_copy(at).wait_send()
        gain_b_copy(at).wait_send()


def hand_over(*refs):
    sources, targets, buffers, (in_sem, out_sem) = refs[:5], refs[5:10], refs[10:15], refs[15:]
    ways = []
    for at, (source, target, buffer) in enumerate(zip(sources, targets, buffers)):
        pieces = 4 if at < 2 else 1
        for piece in range(pieces):
            if len(source.shape) == 3:
                count = source.shape[1] // pieces
                view = (0, pl.ds(piece * count, count))
            else:
                view = (pl.ds(0, 1),)
            ways.append(
                (
                    pltpu.make_async_copy(
                        source.at[view], buffer.at[view], in_sem.at[at * 4 + piece]
                    ),
                    pltpu.make_async_copy(
                        buffer.at[view], target.at[view], out_sem.at[at * 4 + piece]
                    ),
                )
            )
    for inward, _ in ways:
        inward.start()
    for inward, outward in ways:
        inward.wait()
        outward.start()
    for _, outward in ways:
        outward.wait()


def on_device(queries, key_rows, value_rows, upstream, norm_gains, segments):
    any_space = pl.BlockSpec(memory_space=pl.ANY)
    vmem = pl.BlockSpec(memory_space=pltpu.VMEM)
    dma = pltpu.SemaphoreType.DMA
    shapes = [
        jax.ShapeDtypeStruct(queries.shape, BF16),
        jax.ShapeDtypeStruct(queries.shape, BF16),
        jax.ShapeDtypeStruct(key_rows.shape, BF16),
        jax.ShapeDtypeStruct(key_rows.shape, BF16),
        jax.ShapeDtypeStruct(norm_gains.shape, F32),
    ]
    results = pl.pallas_call(
        kernel,
        out_shape=shapes,
        in_specs=[any_space] * 4 + [vmem] * 2,
        out_specs=[any_space] * 4 + [vmem],
        scratch_shapes=[
            pltpu.VMEM((2, ROWS, 2048), BF16),
            pltpu.VMEM((2, ROWS, 2048), BF16),
            pltpu.VMEM((2, 2, SPAN, HEAD_DIM), BF16),
            pltpu.VMEM((2, 2, GROUP * ROWS, HEAD_DIM), BF16),
            pltpu.VMEM((2, SPAN, HEAD_DIM), BF16),
            pltpu.VMEM((2, HEAD_DIM, SPAN), F32),
            pltpu.VMEM((2, ROWS, SEEN), F32),
            pltpu.VMEM((2, 2, HEAD_DIM, SPAN), F32),
            pltpu.VMEM((2, 2, ROWS, 2048), BF16),
            pltpu.VMEM((2, 2, 2, ROWS, HEAD_DIM), BF16),
            pltpu.VMEM((2, 2, 4, HEAD_DIM, PAIR), BF16),
            pltpu.VMEM((2, 2, 4, HEAD_DIM, PAIR), BF16),
            pltpu.VMEM((2, 8, HEAD_DIM), F32),
            pltpu.VMEM((8, 8, HEAD_DIM), F32),
            pltpu.VMEM((8, 8, HEAD_DIM), F32),
            dma((4, 2)),
            dma((4, 2)),
            dma((4, 2)),
            dma((2, 2, 5)),
            dma((2, 2, 5)),
            dma((2, 2, 4)),
            dma((2, 2, 4)),
            dma((2, 2)),
            dma((2, 2)),
            dma((2, 2)),
            dma((2, 2)),
            dma((2, 2)),
            dma((2, 2)),
            dma((8,)),
            dma((8,)),
            dma((8,)),
            dma((8,)),
        ],
        compiler_params=pltpu.CompilerParams(
            collective_id=0, has_side_effects=True, vmem_limit_bytes=60 * 2**20
        ),
        cost_estimate=pl.CostEstimate(
            flops=6 * 10**9, bytes_accessed=5 * 10**6, transcendentals=5 * 10**6
        ),
    )(queries, key_rows, value_rows, upstream, norm_gains, segments)
    return tuple(
        pl.pallas_call(
            hand_over,
            out_shape=shapes,
            in_specs=[any_space] * 5,
            out_specs=[any_space] * 5,
            scratch_shapes=[pltpu.VMEM(one.shape, one.dtype) for one in shapes]
            + [dma((20,)), dma((20,))],
        )(*results)
    )


def solution(mesh):
    rows = P("section", "seq", None)
    whole = P("section", None)
    return jax.shard_map(
        on_device,
        mesh=mesh,
        in_specs=(rows, rows, rows, rows, whole, whole),
        out_specs=(rows, rows, rows, rows, whole),
        check_vma=False,
    )
```

```python
import functools
import math

import jax
import jax.numpy as jnp
from jax import lax
from jax.experimental import pallas as pl
from jax.experimental.pallas import tpu as pltpu
from jax.sharding import PartitionSpec as P

MESH = pl.DeviceIdType.MESH
HEAD_DIM = 128
GROUP = 8
ROWS = 128
PAIR = 2 * ROWS
SLOTS = 5
SPAN = SLOTS * PAIR
SEEN = SPAN - ROWS
EPSILON = 1e-06
FACTOR = 1.0 / math.sqrt(HEAD_DIM)
EXP2_FACTOR = FACTOR * math.log2(math.e)
MASKED = -1e30
F32 = jnp.float32
BF16 = jnp.bfloat16


def matmul(left, right, left_dim, right_dim):
    return lax.dot_general(
        left, right, (((left_dim,), (right_dim,)), ((), ())), preferred_element_type=F32
    )


def unit_rows(raw):
    values = raw.astype(F32)
    inverse = lax.rsqrt(jnp.mean(values * values, axis=-1, keepdims=True) + EPSILON)
    return values * inverse, inverse


def at_slot(slot):
    return pl.ds(pl.multiple_of(slot * PAIR, PAIR), PAIR)


def kernel(
    queries, keys, values, upstream, gains, segments,
    attended, grad_q, grad_k, grad_v, grad_gains,
    q_raw, up_raw, kv_raw, q_normed, k_normed, k_unit_t, bias, acc,
    out_stage, kv_stage, sum_out, sum_in, gain_acc, gain_a, gain_b,
    local_sem, core_send, core_recv, gather_send, gather_recv,
    reduce_send, reduce_recv, out_sem, out_send, out_recv,
    kv_sem, kv_send, kv_recv, ga_send, ga_recv, gb_send, gb_recv,
):
    section = lax.axis_index("section")
    place = lax.axis_index("seq")
    core = place % 2
    col = (place // 2) % 2
    z = place // 4
    mirror = section // 4
    z_count = 8
    other = 1 - core
    gain_q = gains[:, :HEAD_DIM]
    gain_k = gains[:, HEAD_DIM:]

    def device(z_at, col_at, core_at, section_at=None):
        return (section if section_at is None else section_at, (z_at * 2 + col_at) * 2 + core_at)

    sibling = device(z, col, 1 - core)
    across = device(z, 1 - col, core)
    up_z = device((z + 1) % z_count, col, core)
    down_z = device((z + z_count - 1) % z_count, col, core)
    slant_up = device((z + col) % z_count, 1 - col, core)
    slant_down = device((z + z_count + col - 1) % z_count, 1 - col, core)
    slant = device((z + z_count + 2 * col - 1) % z_count, 1 - col, core)

    up_cross = device((z + 1) % z_count, col, other)
    down_cross = device((z + z_count - 1) % z_count, col, other)

    def z_peer(step):
        return device((z + step) % z_count, col, core)

    def square_peer(code):
        flip_m, flip_h, flip_c = code // 4, (code // 2) % 2, code % 2
        return device(
            z,
            1 - col if flip_h else col,
            1 - core if flip_c else core,
            7 - section if flip_m else section,
        )

    barrier = pltpu.get_barrier_semaphore()
    for step in range(1, 8):
        pl.semaphore_signal(barrier, inc=1, device_id=square_peer(step), device_id_type=MESH)
    for step in range(1, 8):
        pl.semaphore_signal(barrier, inc=1, device_id=z_peer(step), device_id_type=MESH)
    for peer in (slant, up_cross, down_cross):
        pl.semaphore_signal(barrier, inc=1, device_id=peer, device_id_type=MESH)

    def remote(src, dst, send, recv, target):
        return pltpu.make_async_remote_copy(
            src_ref=src, dst_ref=dst, send_sem=send, recv_sem=recv,
            device_id=target, device_id_type=MESH,
        )

    def q_columns(core_at, j):
        return pl.ds(pl.multiple_of(core_at * 2048 + j * 1024, 1024), 1024)

    def kv_columns(core_at, j):
        return pl.ds(pl.multiple_of(core_at * 256 + j * 128, 128), 128)

    def token_rows(core_at):
        return pl.ds(pl.multiple_of((SLOTS - 1) * PAIR + core_at * ROWS, ROWS), ROWS)

    def landing(kind, j):
        if kind < 2:
            return kv_raw.at[j, kind, token_rows(core), :]
        return (q_raw, up_raw)[kind - 2].at[core, :, pl.ds(j * 1024, 1024)]

    def leaving(kind, j, core_at):
        if kind < 2:
            return (keys, values)[kind].at[0, :, kv_columns(core_at, j)]
        return (queries, upstream)[kind - 2].at[0, :, q_columns(core_at, j)]

    def own_copy(kind, j):
        return pltpu.make_async_copy(
            leaving(kind, j, core), landing(kind, j), local_sem.at[kind, j]
        )

    def core_copy(kind, j):
        return remote(
            leaving(kind, j, other), landing(kind, j),
            core_send.at[kind, j], core_recv.at[kind, j], sibling,
        )

    def gather_copy(j, kind, step):
        if step < 2:
            source, target_slot, target = 4 - 2 * step, 2 - 2 * step, up_z
        elif step == 2:
            source, target_slot, target = 4 - 2 * col, 3, across
        else:
            source, target_slot, target = 2, 1, slant_up
        return remote(
            kv_raw.at[j, kind, at_slot(source), :],
            kv_raw.at[j, kind, at_slot(target_slot), :],
            gather_send.at[j, kind, step],
            gather_recv.at[j, kind, step],
            target,
        )

    def head_columns(j):
        return [
            slice((j * GROUP + head) * HEAD_DIM, (j * GROUP + head + 1) * HEAD_DIM)
            for head in range(GROUP)
        ]

    def stacked(ref, r, j):
        return jnp.concatenate([ref[r, :, at] for at in head_columns(j)], 0)

    def prepare_queries(j, r):
        unit, _ = unit_rows(stacked(q_raw, r, j))
        q_normed[j, r] = (unit * gain_q).astype(BF16)

    def prepare_keys(j, slot):
        rows = slice(slot * PAIR, (slot + 1) * PAIR)
        unit, _ = unit_rows(kv_raw[j, 0, rows, :])
        k_normed[j, rows, :] = (unit * gain_k).astype(BF16)
        k_unit_t[j, :, rows] = unit.T

    for kind in (2, 0, 1, 3):
        for j in range(2):
            own_copy(kind, j).start()

    pair_at = z * 2 + col
    pieces = []
    for piece in range(SPAN // 128):
        at = jnp.maximum(pair_at * 2 - 8 + piece, 0)
        pieces.append(segments[:, pl.ds(pl.multiple_of(at * 128, 128), 128)].astype(F32))
    row_at = lax.broadcasted_iota(jnp.int32, (ROWS, SEEN), 0)
    key_at = lax.broadcasted_iota(jnp.int32, (ROWS, SEEN), 1)
    diagonal = lax.broadcasted_iota(jnp.int32, (ROWS, ROWS), 0) == lax.broadcasted_iota(
        jnp.int32, (ROWS, ROWS), 1
    )
    for r in range(2):
        row_segments = jnp.sum(jnp.where(diagonal, pieces[8 + r], 0.0), axis=1, keepdims=True)
        key_segments = jnp.concatenate(pieces[r : r + 9], axis=1)
        first_key = 1024 - r * ROWS - (pair_at % 8) * PAIR
        allowed = (
            (key_at <= row_at + 1024) & (key_at >= first_key) & (key_segments == row_segments)
        )
        bias[r] = jnp.where(allowed, 0.0, MASKED)
    acc[...] = jnp.zeros_like(acc)
    gain_acc[...] = jnp.zeros_like(gain_acc)
    for j in range(2):
        own_copy(2, j).wait()
        prepare_queries(j, core)

    def first_copy(kind, cross):
        rows = pl.ds(pl.multiple_of(2 * PAIR + core * ROWS, ROWS), ROWS)
        return remote(
            leaving(kind, 0, other if cross else core),
            kv_raw.at[0, kind, rows, :],
            gather_send.at[0, kind, 4 * cross],
            gather_recv.at[0, kind, 4 * cross],
            up_cross if cross else up_z,
        )

    def enter(j, kind):
        own_copy(kind, j).wait()
        core_copy(kind, j).wait_recv()
        if j == 1:
            gather_copy(j, kind, 0).start()

    def pass_on(j, kind):
        if j == 0:
            first_copy(kind, 0).wait_recv()
            first_copy(kind, 1).wait_recv()
        else:
            gather_copy(j, kind, 0).wait_recv()
        gather_copy(j, kind, 1).start()
        gather_copy(j, kind, 3).start()

    pl.semaphore_wait(barrier, 17)
    for kind in range(2):
        for cross in range(2):
            first_copy(kind, cross).start()
    for j in range(2):
        for kind in range(2):
            core_copy(kind, j).start()
    for j in range(2):
        for kind in range(2, 4):
            core_copy(kind, j).start()
    for kind in range(2):
        enter(0, kind)

        @pl.when(col == 0)
        def _():
            gather_copy(0, kind, 2).start()

    prepare_keys(0, 4)
    pass_on(0, 0)

    @pl.when(col == 1)
    def _():
        gather_copy(0, 0, 2).start()

    enter(1, 0)
    pass_on(0, 1)

    @pl.when(col == 1)
    def _():
        gather_copy(0, 1, 2).start()

    enter(1, 1)
    prepare_keys(0, 2)
    prepare_keys(1, 4)
    core_copy(2, 0).wait_recv()
    prepare_queries(0, other)
    core_copy(2, 1).wait_recv()
    prepare_queries(1, other)

    def reduce_copy(j, kind, step):
        target = (down_z, down_z, across, slant_down)[step]
        return remote(
            sum_out.at[j, kind, step],
            sum_in.at[j, kind, step],
            reduce_send.at[j, kind, step],
            reduce_recv.at[j, kind, step],
            target,
        )

    def send_sum(j, kind, step, slot):
        sum_out[j, kind, step] = acc[j, kind, :, at_slot(slot)].astype(BF16)
        reduce_copy(j, kind, step).start()

    def add_sum(j, kind, step, slot):
        reduce_copy(j, kind, step).wait_recv()
        acc[j, kind, :, at_slot(slot)] += sum_in[j, kind, step].astype(F32)

    def reduce_first(j, kind):
        send_sum(j, kind, 3, 1)
        send_sum(j, kind, 0, 0)
        send_sum(j, kind, 2, 3)

    def reduce_second(j, kind):
        add_sum(j, kind, 3, 2)
        add_sum(j, kind, 0, 2)
        add_sum(j, kind, 2, 4 - 2 * col)
        send_sum(j, kind, 1, 2)

    def kv_copy(kind, j, r):
        target = (grad_k, grad_v)[kind].at[0, :, kv_columns(core, j)]
        if r is core:
            return pltpu.make_async_copy(kv_stage.at[j, kind, r], target, kv_sem.at[j, kind])
        return remote(
            kv_stage.at[j, kind, r], target, kv_send.at[j, kind], kv_recv.at[j, kind], sibling
        )

    def reduce_last(j, kind):
        add_sum(j, kind, 1, 4)
        slot = at_slot(SLOTS - 1)
        result = acc[j, kind, :, slot].T
        if kind == 0:
            k_unit, k_inverse = unit_rows(kv_raw[j, 0, slot, :])
            scaled = result * gain_k
            result = (
                scaled - k_unit * jnp.mean(scaled * k_unit, axis=-1, keepdims=True)
            ) * k_inverse
        kv_stage[j, kind] = result.astype(BF16).reshape(2, ROWS, HEAD_DIM)
        kv_copy(kind, j, other).start()
        kv_copy(kind, j, core).start()

    def out_copy(kind, j, r):
        target = (attended, grad_q)[kind].at[0, :, q_columns(core, j)]
        source = out_stage.at[kind, r, :, pl.ds(j * 1024, 1024)]
        if r is core:
            return pltpu.make_async_copy(source, target, out_sem.at[kind, j])
        return remote(source, target, out_send.at[kind, j], out_recv.at[kind, j], sibling)

    def attend(j, before_values, after_values, after_keys, after_gains):
        both = range(2)
        seen = [slice(r * ROWS, r * ROWS + SEEN) for r in both]
        q = [q_normed[j, r] for r in both]
        k = [k_normed[j, seen[r], :] for r in both]
        scores, d_probs, probs, probs_b, delta, d_scores = ([None, None] for _ in range(6))

        up = v = None

        def softmax(r):
            masked = scores[r].reshape(GROUP, ROWS, SEEN) + bias[r][None]
            masked = masked.reshape(GROUP * ROWS, SEEN)
            top = jnp.max(masked, axis=1, keepdims=True)
            weights = jnp.exp2((masked - top) * EXP2_FACTOR)
            probs[r] = weights * (1.0 / jnp.sum(weights, axis=1, keepdims=True))
            probs_b[r] = probs[r].astype(BF16)

        def output(r):
            out = matmul(probs_b[r], v[r], 1, 0).astype(BF16)
            delta[r] = jnp.sum(up[r].astype(F32) * out.astype(F32), axis=1, keepdims=True)
            for head, at in enumerate(head_columns(j)):
                out_stage[0, r, :, at] = out[head * ROWS : (head + 1) * ROWS]

        def score_gradient(r):
            d_scores[r] = (probs[r] * (d_probs[r] - delta[r]) * FACTOR).astype(BF16)

        def query_gradient(r):
            d_qn = matmul(d_scores[r], k[r], 1, 0).astype(BF16).astype(F32)
            q_unit, q_inverse = unit_rows(stacked(q_raw, r, j))
            gain_acc[0] += jnp.sum((d_qn * q_unit).reshape(ROWS, GROUP, HEAD_DIM), axis=0)
            scaled = d_qn * gain_q
            d_query = (
                (scaled - q_unit * jnp.mean(scaled * q_unit, axis=-1, keepdims=True)) * q_inverse
            ).astype(BF16)
            for head, at in enumerate(head_columns(j)):
                out_stage[1, r, :, at] = d_query[head * ROWS : (head + 1) * ROWS]

        for r in both:
            scores[r] = matmul(q[r], k[r], 1, 1)
        softmax(0)
        before_values()
        up = [stacked(up_raw, r, j) for r in both]
        v = [kv_raw[j, 1, seen[r], :] for r in both]
        d_probs[0] = matmul(up[0], v[0], 1, 1)
        softmax(1)
        output(0)
        score_gradient(0)
        acc[j, 1, :, seen[0]] += matmul(up[0], probs_b[0], 0, 0)
        d_probs[1] = matmul(up[1], v[1], 1, 1)
        output(1)
        acc[j, 1, :, seen[1]] += matmul(up[1], probs_b[1], 0, 0)
        after_values()
        score_gradient(1)
        acc[j, 0, :, seen[0]] += matmul(q[0], d_scores[0], 0, 0)
        acc[j, 0, :, seen[1]] += matmul(q[1], d_scores[1], 0, 0)
        after_keys()
        query_gradient(0)
        query_gradient(1)
        product = acc[j, 0] * k_unit_t[j]
        total = product[:, :128]
        for piece in range(1, SPAN // 128):
            total = total + product[:, piece * 128 : (piece + 1) * 128]
        gain_acc[1] += jnp.sum(total.T.reshape(16, 8, HEAD_DIM), axis=0)
        after_gains()
        for kind in (1, 0):
            out_copy(kind, j, other).start()
            out_copy(kind, j, core).start()

    def arrive(j, kind, slots=()):
        for step in range(1, 4):
            gather_copy(j, kind, step).wait_recv()
        for slot in slots:
            prepare_keys(j, slot)

    def pass_across(kind):
        pass_on(1, kind)
        gather_copy(1, kind, 2).start()

    def first_values():
        own_copy(3, 0).wait()
        core_copy(3, 0).wait_recv()
        pass_across(0)
        arrive(0, 1)

    def second_values():
        own_copy(3, 1).wait()
        core_copy(3, 1).wait_recv()
        arrive(1, 1)

    def gain_a_copy(step):
        return remote(
            gain_a.at[0], gain_a.at[step], ga_send.at[step], ga_recv.at[step], z_peer(step)
        )

    def gain_b_copy(code):
        return remote(
            gain_b.at[0], gain_b.at[code], gb_send.at[code], gb_recv.at[code], square_peer(code)
        )

    def send_gains():
        gain_a[0, 0:1] = jnp.sum(gain_acc[0], axis=0, keepdims=True)
        gain_a[0, 1:2] = jnp.sum(gain_acc[1], axis=0, keepdims=True)
        gain_a[0, 2:8] = jnp.zeros((6, HEAD_DIM), F32)
        for at in range(1, 8):
            gain_a_copy(at).start()

    def nothing():
        pass

    def first_sums():
        reduce_first(0, 1)
        reduce_first(0, 0)

    def value_sums():
        reduce_second(0, 1)
        reduce_first(1, 1)

    def key_sums():
        reduce_first(1, 0)
        reduce_second(0, 0)

    arrive(0, 0, (0, 1, 3))
    attend(0, first_values, lambda: pass_across(1), first_sums, nothing)
    arrive(1, 0, (0, 1, 2, 3))
    attend(1, second_values, value_sums, key_sums, send_gains)
    reduce_last(0, 1)
    reduce_second(1, 1)
    reduce_last(0, 0)
    reduce_second(1, 0)
    for at in range(1, 8):
        gain_a_copy(at).wait_recv()
    terms = gain_a[z % 8]
    for at in range(1, 8):
        terms = terms + gain_a[(z + 8 - at) % 8]
    gain_b[0] = terms
    for at in range(1, 8):
        gain_b_copy(at).start()
    reduce_last(1, 1)
    reduce_last(1, 0)
    for at in range(1, 8):
        gain_b_copy(at).wait_recv()
    sums = []
    for m in range(2):
        total = None
        for h in range(2):
            for c in range(2):
                term = gain_b[((mirror + m) % 2) * 4 + ((col + h) % 2) * 2 + (core + c) % 2]
                total = term if total is None else total + term
        sums.append(total)
    result = sums[0] + sums[1]
    grad_gains[:, :HEAD_DIM] = result[0:1]
    grad_gains[:, HEAD_DIM:] = result[1:2]

    for j in range(2):
        for kind in range(4):
            core_copy(kind, j).wait_send()
        for kind in range(2):
            for at in range(4):
                if j == 0 and at == 0:
                    first_copy(kind, 0).wait_send()
                    first_copy(kind, 1).wait_send()
                else:
                    gather_copy(j, kind, at).wait_send()
                reduce_copy(j, kind, at).wait_send()
            out_copy(kind, j, core).wait()
            out_copy(kind, j, other).wait()
            kv_copy(kind, j, core).wait()
            kv_copy(kind, j, other).wait()
    for at in range(1, 8):
        gain_a_copy(at).wait_send()
        gain_b_copy(at).wait_send()


def on_device(queries, key_rows, value_rows, upstream, norm_gains, segments):
    any_space = pl.BlockSpec(memory_space=pl.ANY)
    vmem = pl.BlockSpec(memory_space=pltpu.VMEM)
    dma = pltpu.SemaphoreType.DMA
    shapes = [
        jax.ShapeDtypeStruct(queries.shape, BF16),
        jax.ShapeDtypeStruct(queries.shape, BF16),
        jax.ShapeDtypeStruct(key_rows.shape, BF16),
        jax.ShapeDtypeStruct(key_rows.shape, BF16),
        jax.ShapeDtypeStruct(norm_gains.shape, F32),
    ]
    results = pl.pallas_call(
        kernel,
        out_shape=[pltpu.VMEM(one.shape, one.dtype) for one in shapes],
        in_specs=[any_space] * 4 + [vmem] * 2,
        out_specs=[vmem] * 5,
        scratch_shapes=[
            pltpu.VMEM((2, ROWS, 2048), BF16),
            pltpu.VMEM((2, ROWS, 2048), BF16),
            pltpu.VMEM((2, 2, SPAN, HEAD_DIM), BF16),
            pltpu.VMEM((2, 2, GROUP * ROWS, HEAD_DIM), BF16),
            pltpu.VMEM((2, SPAN, HEAD_DIM), BF16),
            pltpu.VMEM((2, HEAD_DIM, SPAN), F32),
            pltpu.VMEM((2, ROWS, SEEN), F32),
            pltpu.VMEM((2, 2, HEAD_DIM, SPAN), F32),
            pltpu.VMEM((2, 2, ROWS, 2048), BF16),
            pltpu.VMEM((2, 2, 2, ROWS, HEAD_DIM), BF16),
            pltpu.VMEM((2, 2, 4, HEAD_DIM, PAIR), BF16),
            pltpu.VMEM((2, 2, 4, HEAD_DIM, PAIR), BF16),
            pltpu.VMEM((2, 8, HEAD_DIM), F32),
            pltpu.VMEM((8, 8, HEAD_DIM), F32),
            pltpu.VMEM((8, 8, HEAD_DIM), F32),
            dma((4, 2)),
            dma((4, 2)),
            dma((4, 2)),
            dma((2, 2, 5)),
            dma((2, 2, 5)),
            dma((2, 2, 4)),
            dma((2, 2, 4)),
            dma((2, 2)),
            dma((2, 2)),
            dma((2, 2)),
            dma((2, 2)),
            dma((2, 2)),
            dma((2, 2)),
            dma((8,)),
            dma((8,)),
            dma((8,)),
            dma((8,)),
        ],
        compiler_params=pltpu.CompilerParams(
            collective_id=0, has_side_effects=True, vmem_limit_bytes=56 * 2**20
        ),
        cost_estimate=pl.CostEstimate(
            flops=6 * 10**9, bytes_accessed=5 * 10**6, transcendentals=5 * 10**6
        ),
    )(queries, key_rows, value_rows, upstream, norm_gains, segments)
    return tuple(results)


def solution(mesh):
    rows = P("section", "seq", None)
    whole = P("section", None)
    return jax.shard_map(
        on_device,
        mesh=mesh,
        in_specs=(rows, rows, rows, rows, whole, whole),
        out_specs=(rows, rows, rows, rows, whole),
        check_vma=False,
    )
```

```python
import functools
import math

import jax
import jax.numpy as jnp
from jax import lax
from jax.experimental import pallas as pl
from jax.experimental.pallas import tpu as pltpu
from jax.sharding import PartitionSpec as P

MESH = pl.DeviceIdType.MESH
HEAD_DIM = 128
GROUP = 8
ROWS = 128
PAIR = 2 * ROWS
SLOTS = 5
SPAN = SLOTS * PAIR
SEEN = SPAN - ROWS
EPSILON = 1e-06
FACTOR = 1.0 / math.sqrt(HEAD_DIM)
EXP2_FACTOR = FACTOR * math.log2(math.e)
MASKED = -1e30
F32 = jnp.float32
BF16 = jnp.bfloat16


def matmul(left, right, left_dim, right_dim):
    return lax.dot_general(
        left, right, (((left_dim,), (right_dim,)), ((), ())), preferred_element_type=F32
    )


def unit_rows(raw):
    values = raw.astype(F32)
    inverse = lax.rsqrt(jnp.mean(values * values, axis=-1, keepdims=True) + EPSILON)
    return values * inverse, inverse


def at_slot(slot):
    return pl.ds(pl.multiple_of(slot * PAIR, PAIR), PAIR)


def kernel(
    queries, keys, values, upstream, gains, segments,
    attended, grad_q, grad_k, grad_v, grad_gains,
    q_raw, up_raw, kv_raw, q_normed, k_normed, k_unit_t, bias, acc,
    out_stage, kv_stage, sum_out, sum_in, gain_acc, gain_a, gain_b,
    local_sem, core_send, core_recv, gather_send, gather_recv,
    reduce_send, reduce_recv, out_sem, out_send, out_recv,
    kv_sem, kv_send, kv_recv, ga_send, ga_recv, gb_send, gb_recv,
):
    section = lax.axis_index("section")
    place = lax.axis_index("seq")
    core = place % 2
    col = (place // 2) % 2
    z = place // 4
    mirror = section // 4
    z_count = 8
    other = 1 - core
    gain_q = gains[:, :HEAD_DIM]
    gain_k = gains[:, HEAD_DIM:]

    def device(z_at, col_at, core_at, section_at=None):
        return (section if section_at is None else section_at, (z_at * 2 + col_at) * 2 + core_at)

    sibling = device(z, col, 1 - core)
    across = device(z, 1 - col, core)
    up_z = device((z + 1) % z_count, col, core)
    down_z = device((z + z_count - 1) % z_count, col, core)
    slant_up = device((z + col) % z_count, 1 - col, core)
    slant_down = device((z + z_count + col - 1) % z_count, 1 - col, core)
    slant = device((z + z_count + 2 * col - 1) % z_count, 1 - col, core)

    up_cross = device((z + 1) % z_count, col, other)
    down_cross = device((z + z_count - 1) % z_count, col, other)

    def z_peer(step):
        return device((z + step) % z_count, col, core)

    def square_peer(code):
        flip_m, flip_h, flip_c = code // 4, (code // 2) % 2, code % 2
        return device(
            z,
            1 - col if flip_h else col,
            1 - core if flip_c else core,
            7 - section if flip_m else section,
        )

    barrier = pltpu.get_barrier_semaphore()
    for step in range(1, 8):
        pl.semaphore_signal(barrier, inc=1, device_id=square_peer(step), device_id_type=MESH)
    for step in range(1, 8):
        pl.semaphore_signal(barrier, inc=1, device_id=z_peer(step), device_id_type=MESH)
    for peer in (slant, up_cross, down_cross):
        pl.semaphore_signal(barrier, inc=1, device_id=peer, device_id_type=MESH)

    def remote(src, dst, send, recv, target):
        return pltpu.make_async_remote_copy(
            src_ref=src, dst_ref=dst, send_sem=send, recv_sem=recv,
            device_id=target, device_id_type=MESH,
        )

    def q_columns(core_at, j):
        return pl.ds(pl.multiple_of(core_at * 2048 + j * 1024, 1024), 1024)

    def kv_columns(core_at, j):
        return pl.ds(pl.multiple_of(core_at * 256 + j * 128, 128), 128)

    def token_rows(core_at):
        return pl.ds(pl.multiple_of((SLOTS - 1) * PAIR + core_at * ROWS, ROWS), ROWS)

    def landing(kind, j):
        if kind < 2:
            return kv_raw.at[j, kind, token_rows(core), :]
        return (q_raw, up_raw)[kind - 2].at[core, :, pl.ds(j * 1024, 1024)]

    def leaving(kind, j, core_at):
        if kind < 2:
            return (keys, values)[kind].at[0, :, kv_columns(core_at, j)]
        return (queries, upstream)[kind - 2].at[0, :, q_columns(core_at, j)]

    def own_copy(kind, j):
        return pltpu.make_async_copy(
            leaving(kind, j, core), landing(kind, j), local_sem.at[kind, j]
        )

    def core_copy(kind, j):
        return remote(
            leaving(kind, j, other), landing(kind, j),
            core_send.at[kind, j], core_recv.at[kind, j], sibling,
        )

    def gather_copy(j, kind, step):
        if step < 2:
            source, target_slot, target = 4 - 2 * step, 2 - 2 * step, up_z
        elif step == 2:
            source, target_slot, target = 4 - 2 * col, 3, across
        else:
            source, target_slot, target = 2, 1, slant_up
        return remote(
            kv_raw.at[j, kind, at_slot(source), :],
            kv_raw.at[j, kind, at_slot(target_slot), :],
            gather_send.at[j, kind, step],
            gather_recv.at[j, kind, step],
            target,
        )

    def head_columns(j):
        return [
            slice((j * GROUP + head) * HEAD_DIM, (j * GROUP + head + 1) * HEAD_DIM)
            for head in range(GROUP)
        ]

    def stacked(ref, r, j):
        return jnp.concatenate([ref[r, :, at] for at in head_columns(j)], 0)

    def prepare_queries(j, r):
        unit, _ = unit_rows(stacked(q_raw, r, j))
        q_normed[j, r] = (unit * gain_q).astype(BF16)

    def prepare_keys(j, slot):
        rows = slice(slot * PAIR, (slot + 1) * PAIR)
        unit, _ = unit_rows(kv_raw[j, 0, rows, :])
        k_normed[j, rows, :] = (unit * gain_k).astype(BF16)
        k_unit_t[j, :, rows] = unit.T

    for kind in (2, 0, 1, 3):
        for j in range(2):
            own_copy(kind, j).start()

    def first_copy(kind, cross):
        rows = pl.ds(pl.multiple_of(2 * PAIR + core * ROWS, ROWS), ROWS)
        return remote(
            leaving(kind, 0, other if cross else core),
            kv_raw.at[0, kind, rows, :],
            gather_send.at[0, kind, 4 * cross],
            gather_recv.at[0, kind, 4 * cross],
            up_cross if cross else up_z,
        )

    def enter(j, kind):
        own_copy(kind, j).wait()
        core_copy(kind, j).wait_recv()
        if j == 1:
            gather_copy(j, kind, 0).start()

    def pass_on(j, kind):
        if j == 0:
            first_copy(kind, 0).wait_recv()
            first_copy(kind, 1).wait_recv()
        else:
            gather_copy(j, kind, 0).wait_recv()
        gather_copy(j, kind, 1).start()
        gather_copy(j, kind, 3).start()

    pl.semaphore_wait(barrier, 17)
    for kind in range(2):
        for cross in range(2):
            first_copy(kind, cross).start()
    for j in range(2):
        for kind in range(2):
            core_copy(kind, j).start()
    for j in range(2):
        for kind in range(2, 4):
            core_copy(kind, j).start()
    for kind in range(2):
        enter(0, kind)

        @pl.when(col == 0)
        def _():
            gather_copy(0, kind, 2).start()


    pair_at = z * 2 + col
    pieces = []
    for piece in range(SPAN // 128):
        at = jnp.maximum(pair_at * 2 - 8 + piece, 0)
        pieces.append(segments[:, pl.ds(pl.multiple_of(at * 128, 128), 128)].astype(F32))
    row_at = lax.broadcasted_iota(jnp.int32, (ROWS, SEEN), 0)
    key_at = lax.broadcasted_iota(jnp.int32, (ROWS, SEEN), 1)
    diagonal = lax.broadcasted_iota(jnp.int32, (ROWS, ROWS), 0) == lax.broadcasted_iota(
        jnp.int32, (ROWS, ROWS), 1
    )
    for r in range(2):
        row_segments = jnp.sum(jnp.where(diagonal, pieces[8 + r], 0.0), axis=1, keepdims=True)
        key_segments = jnp.concatenate(pieces[r : r + 9], axis=1)
        first_key = 1024 - r * ROWS - (pair_at % 8) * PAIR
        allowed = (
            (key_at <= row_at + 1024) & (key_at >= first_key) & (key_segments == row_segments)
        )
        bias[r] = jnp.where(allowed, 0.0, MASKED)
    acc[...] = jnp.zeros_like(acc)
    gain_acc[...] = jnp.zeros_like(gain_acc)
    for j in range(2):
        own_copy(2, j).wait()
        prepare_queries(j, core)

    prepare_keys(0, 4)
    pass_on(0, 0)

    @pl.when(col == 1)
    def _():
        gather_copy(0, 0, 2).start()

    enter(1, 0)
    pass_on(0, 1)

    @pl.when(col == 1)
    def _():
        gather_copy(0, 1, 2).start()

    enter(1, 1)
    prepare_keys(0, 2)
    prepare_keys(1, 4)
    core_copy(2, 0).wait_recv()
    prepare_queries(0, other)
    core_copy(2, 1).wait_recv()
    prepare_queries(1, other)

    def reduce_copy(j, kind, step):
        target = (down_z, down_z, across, slant_down)[step]
        return remote(
            sum_out.at[j, kind, step],
            sum_in.at[j, kind, step],
            reduce_send.at[j, kind, step],
            reduce_recv.at[j, kind, step],
            target,
        )

    def send_sum(j, kind, step, slot):
        sum_out[j, kind, step] = acc[j, kind, :, at_slot(slot)].astype(BF16)
        reduce_copy(j, kind, step).start()

    def add_sum(j, kind, step, slot):
        reduce_copy(j, kind, step).wait_recv()
        acc[j, kind, :, at_slot(slot)] += sum_in[j, kind, step].astype(F32)

    def reduce_first(j, kind):
        send_sum(j, kind, 3, 1)
        send_sum(j, kind, 0, 0)
        send_sum(j, kind, 2, 3)

    def reduce_second(j, kind):
        add_sum(j, kind, 3, 2)
        add_sum(j, kind, 0, 2)
        add_sum(j, kind, 2, 4 - 2 * col)
        send_sum(j, kind, 1, 2)

    def kv_copy(kind, j, r):
        target = (grad_k, grad_v)[kind].at[0, :, kv_columns(core, j)]
        if r is core:
            return pltpu.make_async_copy(kv_stage.at[j, kind, r], target, kv_sem.at[j, kind])
        return remote(
            kv_stage.at[j, kind, r], target, kv_send.at[j, kind], kv_recv.at[j, kind], sibling
        )

    def reduce_last(j, kind):
        add_sum(j, kind, 1, 4)
        slot = at_slot(SLOTS - 1)
        result = acc[j, kind, :, slot].T
        if kind == 0:
            k_unit, k_inverse = unit_rows(kv_raw[j, 0, slot, :])
            scaled = result * gain_k
            result = (
                scaled - k_unit * jnp.mean(scaled * k_unit, axis=-1, keepdims=True)
            ) * k_inverse
        kv_stage[j, kind] = result.astype(BF16).reshape(2, ROWS, HEAD_DIM)
        kv_copy(kind, j, other).start()
        kv_copy(kind, j, core).start()

    def out_copy(kind, j, r):
        target = (attended, grad_q)[kind].at[0, :, q_columns(core, j)]
        source = out_stage.at[kind, r, :, pl.ds(j * 1024, 1024)]
        if r is core:
            return pltpu.make_async_copy(source, target, out_sem.at[kind, j])
        return remote(source, target, out_send.at[kind, j], out_recv.at[kind, j], sibling)

    def attend(j, before_values, after_values, after_keys, after_gains):
        both = range(2)
        seen = [slice(r * ROWS, r * ROWS + SEEN) for r in both]
        q = [q_normed[j, r] for r in both]
        k = [k_normed[j, seen[r], :] for r in both]
        scores, d_probs, probs, probs_b, delta, d_scores = ([None, None] for _ in range(6))

        up = v = None

        def softmax(r):
            masked = scores[r].reshape(GROUP, ROWS, SEEN) + bias[r][None]
            masked = masked.reshape(GROUP * ROWS, SEEN)
            top = jnp.max(masked, axis=1, keepdims=True)
            weights = jnp.exp2((masked - top) * EXP2_FACTOR)
            probs[r] = weights * (1.0 / jnp.sum(weights, axis=1, keepdims=True))
            probs_b[r] = probs[r].astype(BF16)

        def output(r):
            out = matmul(probs_b[r], v[r], 1, 0).astype(BF16)
            delta[r] = jnp.sum(up[r].astype(F32) * out.astype(F32), axis=1, keepdims=True)
            for head, at in enumerate(head_columns(j)):
                out_stage[0, r, :, at] = out[head * ROWS : (head + 1) * ROWS]

        def score_gradient(r):
            d_scores[r] = (probs[r] * (d_probs[r] - delta[r]) * FACTOR).astype(BF16)

        def query_gradient(r):
            d_qn = matmul(d_scores[r], k[r], 1, 0).astype(BF16).astype(F32)
            q_unit, q_inverse = unit_rows(stacked(q_raw, r, j))
            gain_acc[0] += jnp.sum((d_qn * q_unit).reshape(ROWS, GROUP, HEAD_DIM), axis=0)
            scaled = d_qn * gain_q
            d_query = (
                (scaled - q_unit * jnp.mean(scaled * q_unit, axis=-1, keepdims=True)) * q_inverse
            ).astype(BF16)
            for head, at in enumerate(head_columns(j)):
                out_stage[1, r, :, at] = d_query[head * ROWS : (head + 1) * ROWS]

        for r in both:
            scores[r] = matmul(q[r], k[r], 1, 1)
        softmax(0)
        before_values()
        up = [stacked(up_raw, r, j) for r in both]
        v = [kv_raw[j, 1, seen[r], :] for r in both]
        d_probs[0] = matmul(up[0], v[0], 1, 1)
        softmax(1)
        output(0)
        score_gradient(0)
        acc[j, 1, :, seen[0]] += matmul(up[0], probs_b[0], 0, 0)
        d_probs[1] = matmul(up[1], v[1], 1, 1)
        output(1)
        acc[j, 1, :, seen[1]] += matmul(up[1], probs_b[1], 0, 0)
        after_values()
        score_gradient(1)
        acc[j, 0, :, seen[0]] += matmul(q[0], d_scores[0], 0, 0)
        acc[j, 0, :, seen[1]] += matmul(q[1], d_scores[1], 0, 0)
        after_keys()
        query_gradient(0)
        query_gradient(1)
        product = acc[j, 0] * k_unit_t[j]
        total = product[:, :128]
        for piece in range(1, SPAN // 128):
            total = total + product[:, piece * 128 : (piece + 1) * 128]
        gain_acc[1] += jnp.sum(total.T.reshape(16, 8, HEAD_DIM), axis=0)
        after_gains()
        for kind in (1, 0):
            out_copy(kind, j, other).start()
            out_copy(kind, j, core).start()

    def arrive(j, kind, slots=()):
        for step in range(1, 4):
            gather_copy(j, kind, step).wait_recv()
        for slot in slots:
            prepare_keys(j, slot)

    def pass_across(kind):
        pass_on(1, kind)
        gather_copy(1, kind, 2).start()

    def first_values():
        own_copy(3, 0).wait()
        core_copy(3, 0).wait_recv()
        pass_across(0)
        arrive(0, 1)

    def second_values():
        own_copy(3, 1).wait()
        core_copy(3, 1).wait_recv()
        arrive(1, 1)

    def gain_a_copy(step):
        return remote(
            gain_a.at[0], gain_a.at[step], ga_send.at[step], ga_recv.at[step], z_peer(step)
        )

    def gain_b_copy(code):
        return remote(
            gain_b.at[0], gain_b.at[code], gb_send.at[code], gb_recv.at[code], square_peer(code)
        )

    def send_gains():
        gain_a[0, 0:1] = jnp.sum(gain_acc[0], axis=0, keepdims=True)
        gain_a[0, 1:2] = jnp.sum(gain_acc[1], axis=0, keepdims=True)
        gain_a[0, 2:8] = jnp.zeros((6, HEAD_DIM), F32)
        for at in range(1, 8):
            gain_a_copy(at).start()

    def nothing():
        pass

    def first_sums():
        reduce_first(0, 1)
        reduce_first(0, 0)

    def value_sums():
        reduce_second(0, 1)
        reduce_first(1, 1)

    def key_sums():
        reduce_first(1, 0)
        reduce_second(0, 0)

    arrive(0, 0, (0, 1, 3))
    attend(0, first_values, lambda: pass_across(1), first_sums, nothing)
    arrive(1, 0, (0, 1, 2, 3))
    attend(1, second_values, value_sums, key_sums, send_gains)
    reduce_last(0, 1)
    reduce_second(1, 1)
    reduce_last(0, 0)
    reduce_second(1, 0)
    for at in range(1, 8):
        gain_a_copy(at).wait_recv()
    terms = gain_a[z % 8]
    for at in range(1, 8):
        terms = terms + gain_a[(z + 8 - at) % 8]
    gain_b[0] = terms
    for at in range(1, 8):
        gain_b_copy(at).start()
    reduce_last(1, 1)
    reduce_last(1, 0)
    for at in range(1, 8):
        gain_b_copy(at).wait_recv()
    sums = []
    for m in range(2):
        total = None
        for h in range(2):
            for c in range(2):
                term = gain_b[((mirror + m) % 2) * 4 + ((col + h) % 2) * 2 + (core + c) % 2]
                total = term if total is None else total + term
        sums.append(total)
    result = sums[0] + sums[1]
    grad_gains[:, :HEAD_DIM] = result[0:1]
    grad_gains[:, HEAD_DIM:] = result[1:2]

    for j in range(2):
        for kind in range(4):
            core_copy(kind, j).wait_send()
        for kind in range(2):
            for at in range(4):
                if j == 0 and at == 0:
                    first_copy(kind, 0).wait_send()
                    first_copy(kind, 1).wait_send()
                else:
                    gather_copy(j, kind, at).wait_send()
                reduce_copy(j, kind, at).wait_send()
            out_copy(kind, j, core).wait()
            out_copy(kind, j, other).wait()
            kv_copy(kind, j, core).wait()
            kv_copy(kind, j, other).wait()
    for at in range(1, 8):
        gain_a_copy(at).wait_send()
        gain_b_copy(at).wait_send()


def on_device(queries, key_rows, value_rows, upstream, norm_gains, segments):
    any_space = pl.BlockSpec(memory_space=pl.ANY)
    vmem = pl.BlockSpec(memory_space=pltpu.VMEM)
    dma = pltpu.SemaphoreType.DMA
    shapes = [
        jax.ShapeDtypeStruct(queries.shape, BF16),
        jax.ShapeDtypeStruct(queries.shape, BF16),
        jax.ShapeDtypeStruct(key_rows.shape, BF16),
        jax.ShapeDtypeStruct(key_rows.shape, BF16),
        jax.ShapeDtypeStruct(norm_gains.shape, F32),
    ]
    results = pl.pallas_call(
        kernel,
        out_shape=[pltpu.VMEM(one.shape, one.dtype) for one in shapes],
        in_specs=[any_space] * 4 + [vmem] * 2,
        out_specs=[vmem] * 5,
        scratch_shapes=[
            pltpu.VMEM((2, ROWS, 2048), BF16),
            pltpu.VMEM((2, ROWS, 2048), BF16),
            pltpu.VMEM((2, 2, SPAN, HEAD_DIM), BF16),
            pltpu.VMEM((2, 2, GROUP * ROWS, HEAD_DIM), BF16),
            pltpu.VMEM((2, SPAN, HEAD_DIM), BF16),
            pltpu.VMEM((2, HEAD_DIM, SPAN), F32),
            pltpu.VMEM((2, ROWS, SEEN), F32),
            pltpu.VMEM((2, 2, HEAD_DIM, SPAN), F32),
            pltpu.VMEM((2, 2, ROWS, 2048), BF16),
            pltpu.VMEM((2, 2, 2, ROWS, HEAD_DIM), BF16),
            pltpu.VMEM((2, 2, 4, HEAD_DIM, PAIR), BF16),
            pltpu.VMEM((2, 2, 4, HEAD_DIM, PAIR), BF16),
            pltpu.VMEM((2, 8, HEAD_DIM), F32),
            pltpu.VMEM((8, 8, HEAD_DIM), F32),
            pltpu.VMEM((8, 8, HEAD_DIM), F32),
            dma((4, 2)),
            dma((4, 2)),
            dma((4, 2)),
            dma((2, 2, 5)),
            dma((2, 2, 5)),
            dma((2, 2, 4)),
            dma((2, 2, 4)),
            dma((2, 2)),
            dma((2, 2)),
            dma((2, 2)),
            dma((2, 2)),
            dma((2, 2)),
            dma((2, 2)),
            dma((8,)),
            dma((8,)),
            dma((8,)),
            dma((8,)),
        ],
        compiler_params=pltpu.CompilerParams(
            collective_id=0, has_side_effects=True, vmem_limit_bytes=56 * 2**20
        ),
        cost_estimate=pl.CostEstimate(
            flops=6 * 10**9, bytes_accessed=5 * 10**6, transcendentals=5 * 10**6
        ),
    )(queries, key_rows, value_rows, upstream, norm_gains, segments)
    return tuple(results)


def solution(mesh):
    rows = P("section", "seq", None)
    whole = P("section", None)
    return jax.shard_map(
        on_device,
        mesh=mesh,
        in_specs=(rows, rows, rows, rows, whole, whole),
        out_specs=(rows, rows, rows, rows, whole),
        check_vma=False,
    )
```
